256 devices in a mesh: slot: 32 (over z, x_hi, core), limb: 4 (over y), ct: 2 (over x_lo).
Axes of the slice: x: 4 (x_hi: 2, x_lo: 2; x = x_hi * 2 + x_lo), y: 4, z: 8, core: 2. Of those that a mesh axis runs over, the one named last changes fastest.
Arguments:
- ciphertexts: float32 [2, 2, 24, 65536], P('ct', None, 'limb', 'slot'), parts along dimension 0, may hold values from -6 to 6
- diagonals: bfloat16 [8, 8, 24, 65536], P(None, None, 'limb', 'slot'), may hold values from -0.75 to 0.75
- baby_keys: bfloat16 [7, 3, 2, 32, 65536], P(None, None, None, 'limb', 'slot'), may hold values from -3.5 to 3.5
- giant_keys: bfloat16 [7, 3, 2, 32, 65536], P(None, None, None, 'limb', 'slot'), may hold values from -3.5 to 3.5
- up_factors: float32 [32, 24], P('limb'), may hold values from -2 to 2
- down_factors: float32 [24, 8], P('limb'), may hold values from -2 to 2
Outputs:
- coefficients: float32 [2, 2, 24, 65536], P('ct', None, 'limb', 'slot'), parts along dimension 0
The draws below stay inside these ranges and needn't reach their ends.
There are 2 independent parts, one for each index of `ct`. The reference program is written for one: setup_inputs(seed, part) draws one part's arguments, and reference() takes and returns one part's arrays. A program takes and returns all parts, laid end to end along the dimension named above; an argument that names none is the same for every part. Nothing has to cross between parts.
All inputs are finite; a program needn't handle non-finite values.
Results may differ from the reference program's by a relative error of at most 0.0003.
Values sent between devices are 32-bit elements; how exact they have to be, the bound alone decides.
No kernel may reach another device: no remote copies, remote signals or barrier semaphores. Data moves between devices by JAX's collectives and lax.ppermute only.
A program may use at most 64 MiB of HBM per device.

```python
import jax
import jax.numpy as jnp
from jax import lax

CTS = 1
SIDE = 256
LIMBS = 24
SPECIAL = 8
DNUM = 3
ALPHA = 8
BABY = 8
GIANT = 8
POINTS = 65536
EXT = 32
Q_DEV = 6
EXT_DEV = 8
STRIDE = 256
N_LIMB = 4


def block_levels(stream_key, shape, shards, low, top_value):
    factor_of, own = 1.0, jax.random.fold_in(stream_key, 6)
    for position, blocks in shards:
        draws = jnp.exp(jax.random.uniform(jax.random.fold_in(own, position), (blocks,), jnp.float32, low / len(shards), top_value / len(shards)))
        factor_of = factor_of * jnp.repeat(draws, shape[position] // blocks).reshape([-1 if axis == position else 1 for axis in range(len(shape))])
    return factor_of


def normal_values(key, extent, scale, most, shards=(), kind=jnp.bfloat16):
    result = jax.random.normal(key, extent, jnp.float32) * scale
    if len(shards) > 0:
        result = block_levels(key, extent, shards, -0.22, 0.18) * result
    return jnp.clip(result, min=-most, max=most).astype(kind)


def setup_inputs(seed: int = 0, part: int = 0) -> dict:
    seeds = jax.random.split(jax.random.key(seed), 7)
    own_keys = jax.random.split(jax.random.fold_in(seeds[6], part), 7)
    ciphertexts = normal_values(own_keys[0], (CTS, 2, LIMBS, POINTS), 1.0, 6.0, ((2, 4), (3, 32)), jnp.float32)
    diagonals = normal_values(seeds[1], (GIANT, BABY, LIMBS, POINTS), (BABY * GIANT) ** -0.5, 0.75, ((2, 4), (3, 32)))
    baby_keys = normal_values(seeds[2], (BABY - 1, DNUM, 2, EXT, POINTS), DNUM ** -0.5, 3.5, ((3, 4), (4, 32)))
    giant_keys = normal_values(seeds[3], (GIANT - 1, DNUM, 2, EXT, POINTS), DNUM ** -0.5, 3.5, ((3, 4), (4, 32)))
    up_factors = normal_values(seeds[4], (EXT, LIMBS), ALPHA ** -0.5, 2.0, ((0, 4),), jnp.float32)
    down_factors = normal_values(seeds[5], (LIMBS, SPECIAL), SPECIAL ** -0.5, 2.0, ((0, 4),), jnp.float32)
    return {"ciphertexts": ciphertexts, "diagonals": diagonals, "baby_keys": baby_keys, "giant_keys": giant_keys, "up_factors": up_factors, "down_factors": down_factors}


TOPMOST_LEVEL = lax.Precision.HIGHEST

def cosine_matrix_entries(side_count):
    freqs = jnp.arange(side_count, dtype=jnp.float32)[:, None]
    slot_positions = jnp.arange(side_count, dtype=jnp.float32)[None, :]
    scaling = jnp.where(freqs == 0, jnp.sqrt(1.0 / side_count), jnp.sqrt(2.0 / side_count))
    return scaling * jnp.cos(jnp.pi * (slot_positions + 0.5) * freqs / side_count)

def transform_whole(values, matrix):
    leading_dims = values.shape[:-1]
    squared = values.reshape(leading_dims + (SIDE, SIDE))
    mixed = jnp.einsum('ka,...ab,cb->...kc', matrix, squared, matrix, precision=TOPMOST_LEVEL)
    return mixed.reshape(leading_dims + (POINTS,))

def raise_whole(second_component, up_factors):
    digit_of = jnp.arange(LIMBS, dtype=jnp.int32) // ALPHA
    digit_mask = (digit_of[None, :] == jnp.arange(DNUM, dtype=jnp.int32)[:, None]).astype(jnp.float32)
    weight_factors = up_factors[None, :, :] * digit_mask[:, None, :]
    return jnp.einsum('irl,aly->airy', weight_factors, second_component, precision=TOPMOST_LEVEL)

def switch_whole(raised, keys, down_factors):
    product = jnp.einsum('cden,dsen->csen', raised, keys.astype(jnp.float32), precision=TOPMOST_LEVEL)
    count = product.shape[0]
    grouped = product.reshape(count, 2, N_LIMB, EXT_DEV, POINTS)
    kept = grouped[:, :, :, :Q_DEV].reshape(count, 2, LIMBS, POINTS)
    spare = grouped[:, :, :, Q_DEV:].reshape(count, 2, SPECIAL, POINTS)
    return kept - jnp.einsum('ls,cusn->culn', down_factors, spare, precision=TOPMOST_LEVEL)

def rotate_switch(pair_values, amount, keys, up_factors, down_factors):
    moved = jnp.roll(pair_values, amount, axis=-1)
    switched = switch_whole(raise_whole(moved[:, 1], up_factors), keys, down_factors)
    return jnp.stack((moved[:, 0] + switched[:, 0], switched[:, 1]), axis=1)

def reference(ciphertexts, diagonals, baby_keys, giant_keys, up_factors, down_factors):
    table = cosine_matrix_entries(SIDE)
    evals = transform_whole(ciphertexts, table)
    babies = [evals]
    for baby_step in range(1, BABY):
        babies.append(rotate_switch(evals, baby_step * STRIDE, baby_keys[baby_step - 1], up_factors, down_factors))
    total = jnp.zeros_like(evals)
    for giant_step in range(GIANT):
        inner = jnp.zeros_like(evals)
        for baby_step in range(BABY):
            inner = inner + diagonals[giant_step, baby_step].astype(jnp.float32) * babies[baby_step]
        if giant_step == 0:
            total = total + inner
        else:
            total = total + rotate_switch(inner, giant_step * BABY * STRIDE, giant_keys[giant_step - 1], up_factors, down_factors)
    return transform_whole(total, table.T)
```

```python
import numpy as np
import jax
import jax.numpy as jnp
import ml_dtypes
from jax import lax
from jax.experimental import pallas as pl
from jax.experimental.pallas import tpu as pltpu
from jax.sharding import PartitionSpec as P

SIDE = 256
DNUM = 3
BABY = 8
GIANT = 8
Q_DEV = 6
LANES = 128
POINTS_DEV = 2048
HALO = 2 * POINTS_DEV
SLOTS = 32
GROUPS = 4
CHUNK = 512
VMEM_BYTES = 48 * 1024 * 1024
F32 = jnp.float32
BF16 = jnp.bfloat16


def split_constant(values):
    high = values.astype(ml_dtypes.bfloat16)
    low = (values - high.astype(np.float64)).astype(ml_dtypes.bfloat16)
    return np.stack([high, low])


def cosine_matrix():
    k = np.arange(SIDE, dtype=np.float64)[:, None]
    n = np.arange(SIDE, dtype=np.float64)[None, :]
    scale = np.where(k == 0, np.sqrt(1.0 / SIDE), np.sqrt(2.0 / SIDE))
    return scale * np.cos(np.pi * (n + 0.5) * k / SIDE)


def lane_orders():
    lane = np.arange(SIDE)
    half, low = lane // LANES, lane % LANES
    block, rest = low // 64, low % 64
    rows = half * 128 + block * 64 + (rest % 8) * 8 + rest // 8
    cols_fwd = half * 128 + (low % 16) * 8 + low // 16
    c = (low // 64) * 8 + low % 8
    k = (low // 8) % 8
    cols_inv = half * 128 + c * 8 + k
    return rows, cols_fwd, cols_inv


def dct_constants():
    c = cosine_matrix()
    rows, cols_fwd, cols_inv = lane_orders()
    return (
        split_constant(c.T[rows]),
        split_constant(c.T[cols_fwd]),
        split_constant(c[rows]),
        split_constant(c[cols_inv]),
    )


def baby_selectors():
    limb_of = np.array([6 * (q // 8) + q % 8 if q % 8 < 6 else -1 for q in range(32)])
    pick = np.zeros((24, 32), np.float32)
    for q in range(32):
        if limb_of[q] >= 0:
            pick[limb_of[q], q] = 1.0
    rows = np.zeros((120, 16), np.float32)
    mask = np.zeros((120, 32), np.float32)
    for d in range(DNUM):
        for e in range(8):
            rows[d * 8 + e, e] = 1.0
            mask[d * 8 + e] = (limb_of >= 0) & (limb_of // 8 == d)
        for g in range(GROUPS):
            for t in range(8):
                row = 24 + (g * 3 + d) * 8 + t
                rows[row, 8 + 2 * g + t % 2] = 1.0
                mask[row] = (limb_of >= 0) & (limb_of // 8 == d)
    return rows, pick, mask


def giant_selectors():
    rows = np.zeros((96, 8), np.float32)
    pick = np.zeros((24, 96), np.float32)
    mask = np.zeros((96, 96), np.float32)
    for j in range(4):
        for d in range(DNUM):
            for e in range(8):
                rows[(j * 3 + d) * 8 + e, e] = 1.0
    for g in range(GROUPS):
        for j in range(4):
            for i in range(Q_DEV):
                limb = 6 * g + i
                pick[limb, g * 24 + j * 6 + i] = 1.0
                d = limb // 8
                mask[(j * 3 + d) * 8 : (j * 3 + d) * 8 + 8, g * 24 + j * 6 + i] = 1.0
    return rows, pick, mask


def exchange(values, lane_bits):
    values = list(values)
    lane = lax.broadcasted_iota(jnp.int32, values[0].shape, values[0].ndim - 1)
    for place, bit in enumerate(reversed(lane_bits)):
        step, span = 1 << place, 1 << bit
        keep = (lane & span) == 0
        for i in range(len(values)):
            if i & step:
                continue
            a, b = values[i], values[i + step]
            values[i] = jnp.where(keep, a, pltpu.roll(b, span, a.ndim - 1))
            values[i + step] = jnp.where(keep, pltpu.roll(a, LANES - span, a.ndim - 1), b)
    return values


def halves(values):
    high = values.astype(BF16)
    return high, (values - high.astype(F32)).astype(BF16)


def matmul(a, b):
    return lax.dot_general(a, b, (((1,), (0,)), ((), ())), preferred_element_type=F32)


def exact_matmul(a, b):
    return lax.dot_general(
        a,
        b,
        (((1,), (0,)), ((), ())),
        precision=lax.Precision.HIGHEST,
        preferred_element_type=F32,
    )


def transform(values, table):
    high, low = halves(values)
    return matmul(high, table[0]) + matmul(low, table[0]) + matmul(high, table[1])


def call(kernel, out_shapes, *args, scratch=(), flops=1000000):
    shapes = [jax.ShapeDtypeStruct(s, F32) for s in out_shapes]
    return pl.pallas_call(
        kernel,
        out_shape=shapes if len(shapes) > 1 else shapes[0],
        scratch_shapes=list(scratch),
        compiler_params=pltpu.CompilerParams(vmem_limit_bytes=VMEM_BYTES),
        cost_estimate=pl.CostEstimate(flops=flops, bytes_accessed=400000, transcendentals=0),
    )(*args)


def special_kernel(keys_ref, up_ref, out_ref):
    out_ref[...] = jnp.zeros_like(out_ref)
    for k in range(BABY - 1):
        for d in range(DNUM):
            for s in range(2):
                rows = keys_ref[k, d, s].astype(F32)[Q_DEV:]
                at = d * 32 + k * 4 + s * 2
                out_ref[at : at + 2, :] = rows
    out_ref[28:30, 0:24] = up_ref[Q_DEV:, :]


def spread_rows(piece, out_ref):
    for h in range(2):
        parts = [piece(p, r * SIDE + h * LANES) for p in range(2) for r in range(8)]
        for c, part in enumerate(exchange(parts, (6, 5, 4, 3))):
            out_ref[h * 16 + c] = part


def rows_kernel(x_ref, out_ref):
    spread_rows(lambda p, at: x_ref[0, p, :, at : at + LANES], out_ref)


def column_transform(in_ref, table_ref, hold_ref):
    hold_ref[...] = jnp.zeros_like(hold_ref)
    for h in range(2):
        parts = exchange([in_ref[h * 16 + s] for s in range(16)], (6, 2, 1, 0))
        for i, part in enumerate(parts):
            hold_ref[i, 0:Q_DEV, h * LANES : (h + 1) * LANES] = part
    result = transform(hold_ref[...].reshape(128, SIDE), table_ref)
    return result.reshape(16, 8, SIDE)


def columns_kernel(in_ref, table_ref, out_ref, hold_ref):
    result = column_transform(in_ref, table_ref, hold_ref)
    lane = lax.broadcasted_iota(jnp.int32, (8, LANES), 1)
    first = (lane & 8) == 0
    for p in range(2):
        pairs = []
        for h in range(2):
            parts = [result[p * 8 + k][:, h * LANES : (h + 1) * LANES] for k in range(8)]
            pairs += exchange(parts, (6, 5, 4))
        for i in range(16):
            out_ref[2 * i + 1, p] = pairs[i][:Q_DEV]
            both = jnp.where(
                first, pltpu.roll(pairs[i - 1], LANES - 8, 1), pltpu.roll(pairs[i], 8, 1)
            )
            out_ref[2 * i, p] = both[:Q_DEV]


def evals_kernel(in_ref, table_ref, e0_ref, e1_ref, e1x_ref, hold_ref):
    hold_ref[...] = jnp.zeros_like(hold_ref)
    for p in range(2):
        for h in range(2):
            parts = exchange([in_ref[h * 16 + c, p] for c in range(16)], (3, 2, 1, 0))
            for row, part in enumerate(parts):
                hold_ref[p * 16 + row, 0:Q_DEV, h * LANES : (h + 1) * LANES] = part
    result = transform(hold_ref[...].reshape(256, SIDE), table_ref).reshape(32, 8, SIDE)
    for row in range(16):
        at = slice(row * SIDE, (row + 1) * SIDE)
        e0_ref[:, at] = result[row][:Q_DEV]
        second = result[16 + row][:Q_DEV]
        e1_ref[:, at] = second
        for g in range(GROUPS):
            e1x_ref[g, :, at] = second


def babies_kernel(
    e1g_ref, e0_ref, e1_ref, up_ref, rows_ref, pick_ref, mask_ref, down_ref, head_ref,
    keys_ref, special_ref, diag_ref,
    send1_ref, send2_ref, send3_ref, four_ref, zero_ref,
    raised_ref, stage_ref, upx_ref,
):
    step = pl.program_id(0)

    @pl.when(step == 0)
    def _():
        upx_ref[0:8, :] = up_ref[...]
        for g in range(GROUPS):
            upx_ref[8 + 2 * g : 10 + 2 * g, :] = head_ref[g, 4:6, 0:24]
        spread = exact_matmul(upx_ref[...], pick_ref[...])
        factors = exact_matmul(rows_ref[...], spread) * mask_ref[...]
        fh, fl = halves(factors)
        lhs = jnp.concatenate([fh, fh, fl], axis=1)
        stage_ref[...] = jnp.zeros_like(stage_ref)
        for g in range(GROUPS):
            stage_ref[8 * g : 8 * g + Q_DEV, :] = e1g_ref[g]
        for part in range(8):
            at = slice(part * 512, (part + 1) * 512)
            eh, el = halves(stage_ref[:, at])
            raised_ref[:, at] = matmul(lhs, jnp.concatenate([eh, el, eh], axis=0))

    upper = lax.broadcasted_iota(jnp.int32, (8, LANES), 0) < 4
    down = down_ref[...]
    columns = [jnp.broadcast_to(down[:, i : i + 1], (Q_DEV, LANES)) for i in range(8)]

    def body(t, carry):
        lane = pl.multiple_of(t * LANES, LANES)
        base = pl.multiple_of(step * CHUNK + t * LANES, LANES)
        here = pl.ds(lane, LANES)

        def view(ref, first, count, k):
            return ref[first : first + count, pl.ds(base + (8 - k) * SIDE, LANES)]

        babies = [(view(e0_ref, 0, Q_DEV, 0), view(e1_ref, 0, Q_DEV, 0))]
        for pair in range(4):
            spare = []
            for g in range(GROUPS):
                total = None
                for d in range(DNUM):
                    at = 24 + (g * 3 + d) * 8
                    k = 2 * pair + 1
                    both = jnp.where(
                        upper, view(raised_ref, at, 8, k), view(raised_ref, at, 8, k + 1)
                    )
                    row = d * 32 + pair * 8
                    term = both * special_ref[g, row : row + 8, here]
                    total = term if total is None else total + term
                spare.append(total)
            for k in (2 * pair + 1, 2 * pair + 2):
                if k == BABY:
                    continue
                views = [view(raised_ref, d * 8, 8, k) for d in range(DNUM)]
                polys = []
                for s in range(2):
                    total = None
                    for d in range(DNUM):
                        term = views[d] * keys_ref[k - 1, d, s, :, here].astype(F32)
                        total = term if total is None else total + term
                    total = total[:Q_DEV]
                    for g in range(GROUPS):
                        for i in range(2):
                            row = ((k - 1) % 2) * 4 + s * 2 + i
                            total = total - columns[2 * g + i] * spare[g][row : row + 1]
                    polys.append(total)
                polys[0] = polys[0] + view(e0_ref, 0, Q_DEV, k)
                babies.append(tuple(polys))
        sends = (None, send1_ref, send2_ref, send3_ref)
        for j in range(GIANT):
            inner = [None, None]
            for k in range(BABY):
                factor = diag_ref[j, k, :, here].astype(F32)
                for s in range(2):
                    term = factor * babies[k][s]
                    inner[s] = term if inner[s] is None else inner[s] + term
            if j % 4 == 0:
                target = zero_ref if j == 0 else four_ref
                target[0, :, here] = inner[0]
                target[1, :, here] = inner[1]
            else:
                at = 6 * (j // 4)
                sends[j % 4][at : at + 6, here] = inner[1]
                sends[j % 4][12 + at : 18 + at, here] = inner[0]
        return carry

    lax.fori_loop(0, CHUNK // LANES, body, 0)


def babies_call(e1g, e0, e1, up, down, keys, special, diagonals):
    rows, pick, mask = baby_selectors()
    head = special[:, 24:32, 0:LANES]
    whole = lambda a: pl.BlockSpec(a.shape, lambda i, n=a.ndim: (0,) * n)
    lanes = lambda *lead: pl.BlockSpec(lead + (CHUNK,), lambda i, n=len(lead): (0,) * n + (i,))
    consts = (e1g, e0, e1, up, rows, pick, mask, down, head)
    outs = [(24, POINTS_DEV)] * 3 + [(2, Q_DEV, POINTS_DEV)] * 2
    return pl.pallas_call(
        babies_kernel,
        grid=(POINTS_DEV // CHUNK,),
        in_specs=[whole(a) for a in consts]
        + [lanes(7, 3, 2, 8), lanes(4, 96), lanes(8, 8, Q_DEV)],
        out_specs=[lanes(24)] * 3 + [lanes(2, Q_DEV)] * 2,
        out_shape=[jax.ShapeDtypeStruct(s, F32) for s in outs],
        scratch_shapes=[
            pltpu.VMEM((120, HALO), F32),
            pltpu.VMEM((32, HALO), F32),
            pltpu.VMEM((16, 24), F32),
        ],
        compiler_params=pltpu.CompilerParams(vmem_limit_bytes=VMEM_BYTES),
        cost_estimate=pl.CostEstimate(flops=40000000, bytes_accessed=6000000, transcendentals=0),
    )(*consts, keys, special, diagonals)


def sort_kernel(got1_ref, got2_ref, got3_ref, four_ref, near_ref, far_ref):
    gots = (got1_ref, got2_ref, got3_ref)
    far_ref[0:6, :] = four_ref[1]
    rest = four_ref[0]
    for r, got in enumerate(gots):
        far_ref[6 + 6 * r : 12 + 6 * r, :] = got[6:12, :]
        rest = rest + got[18:24, :]
        for g in range(GROUPS):
            near_ref[g, 6 * r : 6 * r + 6, :] = got[0:6, :]
    for g in range(GROUPS):
        near_ref[g, 18:24, :] = jnp.zeros((6, POINTS_DEV), F32)
    far_ref[24:30, :] = rest
    far_ref[30:32, :] = jnp.zeros((2, POINTS_DEV), F32)


def giants_kernel(
    near_ref, far_ref, up_ref, rows_ref, pick_ref, mask_ref,
    keys_ref, zero_ref, got1_ref, got2_ref, got3_ref, moved_ref,
    total_ref, spare_ref,
    raised_ref, factor_ref,
):
    step = pl.program_id(0)

    @pl.when(step == 0)
    def _():
        spread = exact_matmul(up_ref[...], pick_ref[...])
        factors = exact_matmul(rows_ref[...], spread) * mask_ref[...]
        fh, fl = halves(factors)
        factor_ref[0] = fh
        factor_ref[1] = fl

    for part, ref in enumerate((near_ref, far_ref)):
        eh, el = halves(ref[...].reshape(96, CHUNK))
        raised_ref[part] = (
            matmul(factor_ref[0], eh) + matmul(factor_ref[0], el) + matmul(factor_ref[1], eh)
        )

    def body(t, carry):
        here = pl.ds(pl.multiple_of(t * LANES, LANES), LANES)
        sums = [None, None]
        for j in range(1, GIANT):
            part, place = (0, j - 1) if j < 4 else (1, j - 4)
            for d in range(DNUM):
                at = (place * 3 + d) * 8
                value = raised_ref[part, at : at + 8, here]
                for s in range(2):
                    term = value * keys_ref[j - 1, d, s, :, here].astype(F32)
                    sums[s] = term if sums[s] is None else sums[s] + term
        first = zero_ref[0, :, here] + moved_ref[24:30, here]
        for got in (got1_ref, got2_ref, got3_ref):
            first = first + got[12:18, here]
        total_ref[0, :, here] = first + sums[0][:Q_DEV]
        total_ref[1, :, here] = zero_ref[1, :, here] + sums[1][:Q_DEV]
        for g in range(GROUPS):
            spare_ref[g, 0:2, here] = sums[0][Q_DEV:]
            spare_ref[g, 2:4, here] = sums[1][Q_DEV:]
        return carry

    lax.fori_loop(0, CHUNK // LANES, body, 0)


def giants_call(near, far, up, keys, zero, gots, moved):
    rows, pick, mask = giant_selectors()
    whole = lambda a: pl.BlockSpec(a.shape, lambda i, n=a.ndim: (0,) * n)
    lanes = lambda *lead: pl.BlockSpec(lead + (CHUNK,), lambda i, n=len(lead): (0,) * n + (i,))
    consts = (up, rows, pick, mask)
    return pl.pallas_call(
        giants_kernel,
        grid=(POINTS_DEV // CHUNK,),
        in_specs=[lanes(4, 24)] * 2
        + [whole(a) for a in consts]
        + [lanes(7, 3, 2, 8), lanes(2, Q_DEV)]
        + [lanes(24)] * 3
        + [lanes(32)],
        out_specs=[lanes(2, Q_DEV), lanes(4, 4)],
        out_shape=[
            jax.ShapeDtypeStruct((2, Q_DEV, POINTS_DEV), F32),
            jax.ShapeDtypeStruct((4, 4, POINTS_DEV), F32),
        ],
        scratch_shapes=[pltpu.VMEM((2, 96, CHUNK), F32), pltpu.VMEM((2, 96, 96), BF16)],
        compiler_params=pltpu.CompilerParams(vmem_limit_bytes=VMEM_BYTES),
        cost_estimate=pl.CostEstimate(flops=40000000, bytes_accessed=4000000, transcendentals=0),
    )(near, far, *consts, keys, zero, *gots, moved)


def lower_kernel(total_ref, spare_ref, down_ref, out_ref):
    down = down_ref[...]
    columns = [jnp.broadcast_to(down[:, i : i + 1], (Q_DEV, LANES)) for i in range(8)]

    def piece(p, at):
        value = total_ref[p, :, at : at + LANES]
        for g in range(GROUPS):
            rows = spare_ref[g, :, at : at + LANES]
            for i in range(2):
                value = value - columns[2 * g + i] * rows[2 * p + i : 2 * p + i + 1]
        return value

    spread_rows(piece, out_ref)


def inverse_columns_kernel(in_ref, table_ref, out_ref, hold_ref):
    result = column_transform(in_ref, table_ref, hold_ref)
    for h in range(2):
        parts = [result[i][:, h * LANES : (h + 1) * LANES] for i in range(16)]
        for g, part in enumerate(exchange(parts, (6, 5, 4, 3))):
            out_ref[h * 16 + g] = part[:Q_DEV]


def inverse_rows_kernel(in_ref, table_ref, out_ref, hold_ref):
    hold_ref[...] = jnp.zeros_like(hold_ref)
    for h in range(2):
        parts = exchange([in_ref[h * 16 + c] for c in range(16)], (6, 2, 1, 0))
        for i, part in enumerate(parts):
            hold_ref[i, 0:Q_DEV, h * LANES : (h + 1) * LANES] = part
    result = transform(hold_ref[...].reshape(128, SIDE), table_ref).reshape(16, 8, SIDE)
    for p in range(2):
        for r in range(8):
            out_ref[0, p, :, r * SIDE : (r + 1) * SIDE] = result[p * 8 + r][:Q_DEV]


def swap(values, axis):
    return lax.all_to_all(values, axis, split_axis=0, concat_axis=0, tiled=True)


def shifted(block, distance):
    route = [(i, (i + distance) % SLOTS) for i in range(SLOTS)]
    return lax.ppermute(block, "slot", route)


def forward(ciphertexts):
    col_fwd, row_fwd, _, _ = dct_constants()
    hold = [pltpu.VMEM((16, 8, SIDE), F32)]
    sent = call(rows_kernel, [(SLOTS, Q_DEV, LANES)], ciphertexts)
    held = swap(sent, "slot")
    sent = call(
        columns_kernel, [(SLOTS, 2, Q_DEV, LANES)], held, col_fwd, scratch=hold, flops=50000000
    )
    held = swap(sent, "slot")
    return call(
        evals_kernel,
        [(Q_DEV, HALO), (Q_DEV, HALO), (GROUPS, Q_DEV, HALO)],
        held,
        row_fwd,
        scratch=[pltpu.VMEM((32, 8, SIDE), F32)],
        flops=100000000,
    )


def inverse(total, spare, down_factors):
    _, _, col_inv, row_inv = dct_constants()
    hold = [pltpu.VMEM((16, 8, SIDE), F32)]
    message = (SLOTS, Q_DEV, LANES)
    sent = call(lower_kernel, [message], total, spare, down_factors)
    held = swap(sent, "slot")
    sent = call(inverse_columns_kernel, [message], held, col_inv, scratch=hold, flops=50000000)
    held = swap(sent, "slot")
    return call(
        inverse_rows_kernel,
        [(1, 2, Q_DEV, POINTS_DEV)],
        held,
        row_inv,
        scratch=hold,
        flops=50000000,
    )


def per_device(ciphertexts, diagonals, baby_keys, giant_keys, up_factors, down_factors):
    special = call(special_kernel, [(96, POINTS_DEV)], baby_keys, up_factors)
    special = lax.all_gather(special, "limb", axis=0)
    e0, e1, e1x = forward(ciphertexts)
    e1g = swap(e1x, "limb")
    send1, send2, send3, four, zero = babies_call(
        e1g, e0, e1, up_factors, down_factors, baby_keys, special, diagonals
    )
    gots = [shifted(send, r + 1) for r, send in enumerate((send1, send2, send3))]
    near, far = call(
        sort_kernel, [(GROUPS, 24, POINTS_DEV), (32, POINTS_DEV)], *gots, four, flops=10000
    )
    moved = shifted(far, 4)
    near = swap(near, "limb")
    far = swap(jnp.broadcast_to(moved[None, :24], (GROUPS, 24, POINTS_DEV)), "limb")
    total, spare = giants_call(near, far, up_factors, giant_keys, zero, gots, moved)
    return inverse(total, swap(spare, "limb"), down_factors)


def solution(mesh):
    placed = (
        P("ct", None, "limb", "slot"),
        P(None, None, "limb", "slot"),
        P(None, None, None, "limb", "slot"),
        P(None, None, None, "limb", "slot"),
        P("limb", None),
        P("limb", None),
    )
    return jax.shard_map(
        per_device,
        mesh=mesh,
        in_specs=placed,
        out_specs=P("ct", None, "limb", "slot"),
        check_vma=False,
    )
```

```python
import numpy as np
import jax
import jax.numpy as jnp
import ml_dtypes
from jax import lax
from jax.experimental import pallas as pl
from jax.experimental.pallas import tpu as pltpu
from jax.sharding import PartitionSpec as P

SIDE = 256
DNUM = 3
BABY = 8
GIANT = 8
Q_DEV = 6
LANES = 128
POINTS_DEV = 2048
HALO = 2 * POINTS_DEV
SLOTS = 32
GROUPS = 4
CHUNK = 512
VMEM_BYTES = 8 * 1024 * 1024
F32 = jnp.float32
BF16 = jnp.bfloat16


def split_constant(values):
    high = values.astype(ml_dtypes.bfloat16)
    low = (values - high.astype(np.float64)).astype(ml_dtypes.bfloat16)
    return np.stack([high, low])


def cosine_matrix():
    k = np.arange(SIDE, dtype=np.float64)[:, None]
    n = np.arange(SIDE, dtype=np.float64)[None, :]
    scale = np.where(k == 0, np.sqrt(1.0 / SIDE), np.sqrt(2.0 / SIDE))
    return scale * np.cos(np.pi * (n + 0.5) * k / SIDE)


def lane_orders():
    lane = np.arange(SIDE)
    half, low = lane // LANES, lane % LANES
    block, rest = low // 64, low % 64
    rows = half * 128 + block * 64 + (rest % 8) * 8 + rest // 8
    cols_fwd = half * 128 + (low % 16) * 8 + low // 16
    c = (low // 64) * 8 + low % 8
    k = (low // 8) % 8
    cols_inv = half * 128 + c * 8 + k
    return rows, cols_fwd, cols_inv


def dct_constants():
    c = cosine_matrix()
    rows, cols_fwd, cols_inv = lane_orders()
    return (
        split_constant(c.T[rows]),
        split_constant(c.T[cols_fwd]),
        split_constant(c[rows]),
        split_constant(c[cols_inv]),
    )


def exchange(values, bits, axis=1):
    values = list(values)
    size = values[0].shape[axis]
    index = lax.broadcasted_iota(jnp.int32, values[0].shape, axis)
    for place, bit in enumerate(reversed(bits)):
        step, span = 1 << place, 1 << bit
        keep = (index & span) == 0
        for i in range(len(values)):
            if i & step:
                continue
            a, b = values[i], values[i + step]
            values[i] = jnp.where(keep, a, pltpu.roll(b, span, axis))
            values[i + step] = jnp.where(keep, pltpu.roll(a, size - span, axis), b)
    return values


def halves(values):
    high = values.astype(BF16)
    return high, (values - high.astype(F32)).astype(BF16)


def matmul(a, b):
    return lax.dot_general(a, b, (((1,), (0,)), ((), ())), preferred_element_type=F32)


def exact_matmul(a, b):
    return lax.dot_general(
        a,
        b,
        (((1,), (0,)), ((), ())),
        precision=lax.Precision.HIGHEST,
        preferred_element_type=F32,
    )


def transform(values, table):
    high, low = halves(values)
    return matmul(high, table[0]) + matmul(low, table[0]) + matmul(high, table[1])


def call(kernel, out_shapes, *args, scratch=(), flops=1000000):
    shapes = [jax.ShapeDtypeStruct(s, F32) for s in out_shapes]
    return pl.pallas_call(
        kernel,
        out_shape=shapes if len(shapes) > 1 else shapes[0],
        scratch_shapes=list(scratch),
        compiler_params=pltpu.CompilerParams(vmem_limit_bytes=VMEM_BYTES),
        cost_estimate=pl.CostEstimate(flops=flops, bytes_accessed=400000, transcendentals=0),
    )(*args)


def group_of(place_ref, m):
    return (place_ref[0] - m) & 3


def down_columns(place_ref, down_ref):
    down = down_ref[...]
    lane = lax.broadcasted_iota(jnp.int32, down.shape, 1)
    columns = []
    for m in range(GROUPS):
        for i in range(2):
            pick = jnp.where(lane == 2 * group_of(place_ref, m) + i, down, 0.0)
            column = jnp.sum(pick, axis=1, keepdims=True)
            columns.append(jnp.broadcast_to(column, (Q_DEV, LANES)))
    return columns


def lowered(kept, rows, columns):
    total = kept
    for g in range(GROUPS):
        for i in range(2):
            total = total - columns[2 * g + i] * rows(g, i)
    return total


def spread_rows(piece, out_ref):
    for h in range(2):
        parts = [piece(p, r * SIDE + h * LANES) for p in range(2) for r in range(8)]
        for c, part in enumerate(exchange(parts, (6, 5, 4, 3))):
            out_ref[h * 16 + c] = part


def rows_kernel(x_ref, out_ref):
    spread_rows(lambda p, at: x_ref[0, p, :, at : at + LANES], out_ref)


def column_transform(in_ref, table_ref, hold_ref):
    hold_ref[...] = jnp.zeros_like(hold_ref)
    for h in range(2):
        parts = exchange([in_ref[h * 16 + s] for s in range(16)], (6, 2, 1, 0))
        for i, part in enumerate(parts):
            hold_ref[i, 0:Q_DEV, h * LANES : (h + 1) * LANES] = part
    result = transform(hold_ref[...].reshape(128, SIDE), table_ref)
    return result.reshape(16, 8, SIDE)


def columns_kernel(in_ref, table_ref, out_ref, hold_ref):
    result = column_transform(in_ref, table_ref, hold_ref)
    lane = lax.broadcasted_iota(jnp.int32, (8, LANES), 1)
    first = (lane & 8) == 0
    for p in range(2):
        pairs = []
        for h in range(2):
            parts = [result[p * 8 + k][:, h * LANES : (h + 1) * LANES] for k in range(8)]
            pairs += exchange(parts, (6, 5, 4))
        for i in range(16):
            out_ref[2 * i + 1, p] = pairs[i][:Q_DEV]
            both = jnp.where(
                first, pltpu.roll(pairs[i - 1], LANES - 8, 1), pltpu.roll(pairs[i], 8, 1)
            )
            out_ref[2 * i, p] = both[:Q_DEV]


def evals_kernel(in_ref, table_ref, e0_ref, e1_ref, hold_ref):
    hold_ref[...] = jnp.zeros_like(hold_ref)
    for p in range(2):
        for h in range(2):
            parts = exchange([in_ref[h * 16 + c, p] for c in range(16)], (3, 2, 1, 0))
            for row, part in enumerate(parts):
                hold_ref[p * 16 + row, 0:Q_DEV, h * LANES : (h + 1) * LANES] = part
    result = transform(hold_ref[...].reshape(256, SIDE), table_ref).reshape(32, 8, SIDE)
    for row in range(16):
        at = slice(row * SIDE, (row + 1) * SIDE)
        e0_ref[:, at] = result[row][:Q_DEV]
        e1_ref[:, at] = result[16 + row][:Q_DEV]


def products_kernel(
    place_ref, e1a_ref, e1b_ref, e1c_ref, e1d_ref, up_ref, keys_ref,
    kept_ref, spare_ref, raised_ref, stage_ref,
):
    step = pl.program_id(0)

    @pl.when(step == 0)
    def _():
        iota = lambda shape, axis: lax.broadcasted_iota(jnp.int32, shape, axis)

        def limb(q):
            group = group_of(place_ref, q >> 3)
            return jnp.where((q & 7) < Q_DEV, 6 * group + (q & 7), -1)

        pick = (iota((24, 32), 0) == limb(iota((24, 32), 1))).astype(F32)
        spread = exact_matmul(up_ref[...], pick)
        digit = limb(iota((8, 32), 1)) >> 3
        factors = jnp.concatenate(
            [jnp.where(digit == d, spread, 0.0) for d in range(DNUM)], axis=0
        )
        fh, fl = halves(factors)
        lhs = jnp.concatenate([fh, fh, fl], axis=1)
        stage_ref[...] = jnp.zeros_like(stage_ref)
        for m, ref in enumerate((e1a_ref, e1b_ref, e1c_ref, e1d_ref)):
            stage_ref[8 * m : 8 * m + Q_DEV, :] = ref[...]
        for part in range(8):
            at = slice(part * 512, (part + 1) * 512)
            eh, el = halves(stage_ref[:, at])
            raised_ref[:, at] = matmul(lhs, jnp.concatenate([eh, el, eh], axis=0))

    def body(t, carry):
        base = pl.multiple_of(step * CHUNK + t * LANES, LANES)
        here = pl.ds(pl.multiple_of(t * LANES, LANES), LANES)
        for k in range(1, BABY):
            at = pl.ds(base + (8 - k) * SIDE, LANES)
            views = [raised_ref[d * 8 : d * 8 + 8, at] for d in range(DNUM)]
            for s in range(2):
                total = None
                for d in range(DNUM):
                    term = views[d] * keys_ref[k - 1, d, s, :, here].astype(F32)
                    total = term if total is None else total + term
                unit = 2 * (k - 1) + s
                kept_ref[unit, :, here] = total
                spare_ref[2 * unit : 2 * unit + 2, here] = total[Q_DEV:]
        return carry

    lax.fori_loop(0, CHUNK // LANES, body, 0)


def babies_kernel(
    place_ref, kept_ref, spare0_ref, spare1_ref, spare2_ref, spare3_ref,
    e0_ref, e1_ref, down_ref, diag_ref,
    send1_ref, send2_ref, send3_ref, four_ref, zero_ref,
):
    step = pl.program_id(0)
    columns = down_columns(place_ref, down_ref)
    spares = (spare0_ref, spare1_ref, spare2_ref, spare3_ref)

    def body(t, carry):
        base = pl.multiple_of(step * CHUNK + t * LANES, LANES)
        here = pl.ds(pl.multiple_of(t * LANES, LANES), LANES)
        own = pl.ds(base + POINTS_DEV, LANES)
        babies = [(e0_ref[:, own], e1_ref[:, own])]
        for k in range(1, BABY):
            polys = []
            for s in range(2):
                unit = 2 * (k - 1) + s
                rows = lambda m, i: spares[m][2 * unit + i : 2 * unit + i + 1, here]
                polys.append(lowered(kept_ref[unit, 0:Q_DEV, here], rows, columns))
            polys[0] = polys[0] + e0_ref[:, pl.ds(base + (8 - k) * SIDE, LANES)]
            babies.append(tuple(polys))
        sends = (None, send1_ref, send2_ref, send3_ref)
        for j in range(GIANT):
            inner = [None, None]
            for k in range(BABY):
                factor = diag_ref[j, k, :, here].astype(F32)
                for s in range(2):
                    term = factor * babies[k][s]
                    inner[s] = term if inner[s] is None else inner[s] + term
            if j % 4 == 0:
                target = zero_ref if j == 0 else four_ref
                target[0, :, here] = inner[0]
                target[1, :, here] = inner[1]
            else:
                at = 6 * (j // 4)
                sends[j % 4][at : at + 6, here] = inner[1]
                sends[j % 4][12 + at : 18 + at, here] = inner[0]
        return carry

    lax.fori_loop(0, CHUNK // LANES, body, 0)


def whole(a):
    return pl.BlockSpec(a.shape, lambda i, n=a.ndim: (0,) * n)


def lanes(*lead):
    return pl.BlockSpec(lead + (CHUNK,), lambda i, n=len(lead): (0,) * n + (i,))


PLACE = pl.BlockSpec(memory_space=pltpu.SMEM)


def products_call(place, evals, up, keys):
    return pl.pallas_call(
        products_kernel,
        grid=(POINTS_DEV // CHUNK,),
        in_specs=[PLACE] + [whole(e) for e in evals] + [whole(up), lanes(7, 3, 2, 8)],
        out_specs=[lanes(14, 8), lanes(28)],
        out_shape=[
            jax.ShapeDtypeStruct((14, 8, POINTS_DEV), F32),
            jax.ShapeDtypeStruct((28, POINTS_DEV), F32),
        ],
        scratch_shapes=[pltpu.VMEM((24, HALO), F32), pltpu.VMEM((32, HALO), F32)],
        compiler_params=pltpu.CompilerParams(vmem_limit_bytes=VMEM_BYTES),
        cost_estimate=pl.CostEstimate(flops=40000000, bytes_accessed=4000000, transcendentals=0),
    )(place, *evals, up, keys)


def babies_call(place, kept, spares, e0, e1, down, diagonals):
    outs = [(24, POINTS_DEV)] * 3 + [(2, Q_DEV, POINTS_DEV)] * 2
    return pl.pallas_call(
        babies_kernel,
        grid=(POINTS_DEV // CHUNK,),
        in_specs=[PLACE, lanes(14, 8)]
        + [lanes(28)] * 4
        + [whole(a) for a in (e0, e1, down)]
        + [lanes(8, 8, Q_DEV)],
        out_specs=[lanes(24)] * 3 + [lanes(2, Q_DEV)] * 2,
        out_shape=[jax.ShapeDtypeStruct(s, F32) for s in outs],
        compiler_params=pltpu.CompilerParams(vmem_limit_bytes=VMEM_BYTES),
        cost_estimate=pl.CostEstimate(flops=40000000, bytes_accessed=6000000, transcendentals=0),
    )(place, kept, *spares, e0, e1, down, diagonals)


def sort_kernel(got1_ref, got2_ref, got3_ref, four_ref, near_ref, far_ref, rest_ref):
    gots = (got1_ref, got2_ref, got3_ref)
    far_ref[0:6, :] = four_ref[1]
    rest = four_ref[0]
    for r, got in enumerate(gots):
        near_ref[6 * r : 6 * r + 6, :] = got[0:6, :]
        far_ref[6 + 6 * r : 12 + 6 * r, :] = got[6:12, :]
        rest = rest + got[18:24, :]
    near_ref[18:24, :] = jnp.zeros((6, POINTS_DEV), F32)
    rest_ref[...] = rest


def giants_kernel(
    place_ref, near0_ref, near1_ref, near2_ref, near3_ref,
    far0_ref, far1_ref, far2_ref, far3_ref, up_ref, keys_ref,
    zero_ref, got1_ref, got2_ref, got3_ref, moved_ref,
    total_ref, spare_ref,
    raised_ref, factor_ref,
):
    step = pl.program_id(0)

    @pl.when(step == 0)
    def _():
        iota = lambda shape, axis: lax.broadcasted_iota(jnp.int32, shape, axis)

        def source(q):
            block = (q >= 24).astype(jnp.int32) + (q >= 48) + (q >= 72)
            rest = q - 24 * block
            giant = (rest * 43) >> 8
            return giant, 6 * group_of(place_ref, block) + rest - 6 * giant

        pick = (iota((24, 96), 0) == source(iota((24, 96), 1))[1]).astype(F32)
        spread = exact_matmul(up_ref[...], pick)
        held, limb = source(iota((8, 96), 1))
        for j in range(4):
            parts = [
                jnp.where((held == j) & ((limb >> 3) == d), spread, 0.0) for d in range(DNUM)
            ]
            at = slice(j * 24, j * 24 + 24)
            fh, fl = halves(jnp.concatenate(parts, axis=0))
            factor_ref[0, at], factor_ref[1, at] = fh.astype(F32), fl.astype(F32)

    fh, fl = factor_ref[0].astype(BF16), factor_ref[1].astype(BF16)
    nears = (near0_ref, near1_ref, near2_ref, near3_ref)
    fars = (far0_ref, far1_ref, far2_ref, far3_ref)
    for part, refs in enumerate((nears, fars)):
        eh, el = halves(jnp.concatenate([ref[...] for ref in refs], axis=0))
        raised_ref[part] = matmul(fh, eh) + matmul(fh, el) + matmul(fl, eh)

    def body(t, carry):
        here = pl.ds(pl.multiple_of(t * LANES, LANES), LANES)
        sums = [None, None]
        for j in range(1, GIANT):
            for d in range(DNUM):
                at = (j - 1 if j < 4 else j - 4) * 24 + d * 8
                value = raised_ref[j // 4, at : at + 8, here]
                for s in range(2):
                    term = value * keys_ref[j - 1, d, s, :, here].astype(F32)
                    sums[s] = term if sums[s] is None else sums[s] + term
        first = zero_ref[0, :, here] + moved_ref[:, here]
        for got in (got1_ref, got2_ref, got3_ref):
            first = first + got[12:18, here]
        total_ref[0, :, here] = first + sums[0][:Q_DEV]
        total_ref[1, :, here] = zero_ref[1, :, here] + sums[1][:Q_DEV]
        spare_ref[0:2, here] = sums[0][Q_DEV:]
        spare_ref[2:4, here] = sums[1][Q_DEV:]
        return carry

    lax.fori_loop(0, CHUNK // LANES, body, 0)


def giants_call(place, nears, fars, up, keys, zero, gots, moved):
    return pl.pallas_call(
        giants_kernel,
        grid=(POINTS_DEV // CHUNK,),
        in_specs=[PLACE]
        + [lanes(24)] * 8
        + [whole(up), lanes(7, 3, 2, 8), lanes(2, Q_DEV)]
        + [lanes(24)] * 3
        + [lanes(Q_DEV)],
        out_specs=[lanes(2, Q_DEV), lanes(4)],
        out_shape=[
            jax.ShapeDtypeStruct((2, Q_DEV, POINTS_DEV), F32),
            jax.ShapeDtypeStruct((4, POINTS_DEV), F32),
        ],
        scratch_shapes=[pltpu.VMEM((2, 96, CHUNK), F32), pltpu.VMEM((2, 96, 96), F32)],
        compiler_params=pltpu.CompilerParams(vmem_limit_bytes=VMEM_BYTES),
        cost_estimate=pl.CostEstimate(flops=40000000, bytes_accessed=4000000, transcendentals=0),
    )(place, *nears, *fars, up, keys, zero, *gots, moved)


def lower_kernel(
    place_ref, total_ref, spare0_ref, spare1_ref, spare2_ref, spare3_ref, down_ref, out_ref
):
    columns = down_columns(place_ref, down_ref)
    spares = (spare0_ref, spare1_ref, spare2_ref, spare3_ref)

    def piece(p, at):
        rows = lambda m, i: spares[m][2 * p + i : 2 * p + i + 1, at : at + LANES]
        return lowered(total_ref[p, :, at : at + LANES], rows, columns)

    spread_rows(piece, out_ref)


def lower_call(place, total, spares, down):
    out = (SLOTS, Q_DEV, LANES)
    return pl.pallas_call(
        lower_kernel,
        in_specs=[PLACE] + [pl.BlockSpec(memory_space=pltpu.VMEM)] * 6,
        out_specs=pl.BlockSpec(memory_space=pltpu.VMEM),
        out_shape=jax.ShapeDtypeStruct(out, F32),
        compiler_params=pltpu.CompilerParams(vmem_limit_bytes=VMEM_BYTES),
        cost_estimate=pl.CostEstimate(flops=1000000, bytes_accessed=400000, transcendentals=0),
    )(place, total, *spares, down)


def inverse_columns_kernel(in_ref, table_ref, out_ref, hold_ref):
    result = column_transform(in_ref, table_ref, hold_ref)
    for h in range(2):
        parts = [result[i][:, h * LANES : (h + 1) * LANES] for i in range(16)]
        for g, part in enumerate(exchange(parts, (6, 5, 4, 3))):
            out_ref[h * 16 + g] = part[:Q_DEV]


def inverse_rows_kernel(in_ref, table_ref, out_ref, hold_ref):
    hold_ref[...] = jnp.zeros_like(hold_ref)
    for h in range(2):
        parts = exchange([in_ref[h * 16 + c] for c in range(16)], (6, 2, 1, 0))
        for i, part in enumerate(parts):
            hold_ref[i, 0:Q_DEV, h * LANES : (h + 1) * LANES] = part
    result = transform(hold_ref[...].reshape(128, SIDE), table_ref).reshape(16, 8, SIDE)
    for p in range(2):
        for r in range(8):
            out_ref[0, p, :, r * SIDE : (r + 1) * SIDE] = result[p * 8 + r][:Q_DEV]


def swap(values, axis):
    return lax.all_to_all(values, axis, split_axis=0, concat_axis=0, tiled=True)


def shifted(block, distance):
    route = [(i, (i + distance) % SLOTS) for i in range(SLOTS)]
    return lax.ppermute(block, "slot", route)


def forward(ciphertexts):
    col_fwd, row_fwd, _, _ = dct_constants()
    hold = [pltpu.VMEM((16, 8, SIDE), F32)]
    sent = call(rows_kernel, [(SLOTS, Q_DEV, LANES)], ciphertexts)
    held = swap(sent, "slot")
    sent = call(
        columns_kernel, [(SLOTS, 2, Q_DEV, LANES)], held, col_fwd, scratch=hold, flops=50000000
    )
    held = swap(sent, "slot")
    return call(
        evals_kernel,
        [(Q_DEV, HALO), (Q_DEV, HALO)],
        held,
        row_fwd,
        scratch=[pltpu.VMEM((32, 8, SIDE), F32)],
        flops=100000000,
    )


def inverse(sent):
    _, _, col_inv, row_inv = dct_constants()
    hold = [pltpu.VMEM((16, 8, SIDE), F32)]
    held = swap(sent, "slot")
    sent = call(
        inverse_columns_kernel,
        [(SLOTS, Q_DEV, LANES)],
        held,
        col_inv,
        scratch=hold,
        flops=50000000,
    )
    held = swap(sent, "slot")
    return call(
        inverse_rows_kernel,
        [(1, 2, Q_DEV, POINTS_DEV)],
        held,
        row_inv,
        scratch=hold,
        flops=50000000,
    )


def gathered(block):
    routes = [[(i, (i + m) % GROUPS) for i in range(GROUPS)] for m in range(GROUPS)]
    return [block] + [lax.ppermute(block, "limb", routes[m]) for m in range(1, GROUPS)]


def per_device(ciphertexts, diagonals, baby_keys, giant_keys, up, down):
    place = lax.axis_index("limb").astype(jnp.int32).reshape(1)
    e0, e1 = forward(ciphertexts)
    kept, spare = products_call(place, gathered(e1), up, baby_keys)
    *sends, four, zero = babies_call(place, kept, gathered(spare), e0, e1, down, diagonals)
    gots = [shifted(send, r + 1) for r, send in enumerate(sends)]
    near, far, rest = call(
        sort_kernel,
        [(24, POINTS_DEV), (24, POINTS_DEV), (Q_DEV, POINTS_DEV)],
        *gots,
        four,
        flops=10000,
    )
    far, rest = shifted(far, 4), shifted(rest, 4)
    total, spare = giants_call(
        place, gathered(near), gathered(far), up, giant_keys, zero, gots, rest
    )
    return inverse(lower_call(place, total, gathered(spare), down))


def solution(mesh):
    placed = (
        P("ct", None, "limb", "slot"),
        P(None, None, "limb", "slot"),
        P(None, None, None, "limb", "slot"),
        P(None, None, None, "limb", "slot"),
        P("limb", None),
        P("limb", None),
    )
    return jax.shard_map(
        per_device,
        mesh=mesh,
        in_specs=placed,
        out_specs=P("ct", None, "limb", "slot"),
        check_vma=False,
    )
```

```python
import functools

import numpy as np
import jax
import jax.numpy as jnp
import ml_dtypes
from jax import lax
from jax.experimental import pallas as pl
from jax.experimental.pallas import tpu as pltpu
from jax.sharding import PartitionSpec as P

SIDE = 256
DNUM = 3
BABY = 8
GIANT = 8
Q_DEV = 6
LANES = 128
POINTS_DEV = 2048
HALO = 2 * POINTS_DEV
SLOTS = 32
GROUPS = 4
CHUNK = 1024
VMEM_BYTES = 14 * 1024 * 1024
F32 = jnp.float32
BF16 = jnp.bfloat16


def split_constant(values):
    high = values.astype(ml_dtypes.bfloat16)
    low = (values - high.astype(np.float64)).astype(ml_dtypes.bfloat16)
    return np.stack([high, low])


def cosine_matrix():
    k = np.arange(SIDE, dtype=np.float64)[:, None]
    n = np.arange(SIDE, dtype=np.float64)[None, :]
    scale = np.where(k == 0, np.sqrt(1.0 / SIDE), np.sqrt(2.0 / SIDE))
    return scale * np.cos(np.pi * (n + 0.5) * k / SIDE)


def lane_orders():
    lane = np.arange(SIDE)
    half, low = lane // LANES, lane % LANES
    block, rest = low // 64, low % 64
    rows = half * 128 + block * 64 + (rest % 8) * 8 + rest // 8
    cols_fwd = half * 128 + (low % 16) * 8 + low // 16
    c = (low // 64) * 8 + low % 8
    k = (low // 8) % 8
    cols_inv = half * 128 + c * 8 + k
    return rows, cols_fwd, cols_inv


def dct_constants():
    c = cosine_matrix()
    rows, cols_fwd, cols_inv = lane_orders()
    return (
        split_constant(c.T[rows]),
        split_constant(c.T[cols_fwd]),
        split_constant(c[rows]),
        split_constant(c[cols_inv]),
    )


def exchange(values, bits, axis=1):
    values = list(values)
    size = values[0].shape[axis]
    index = lax.broadcasted_iota(jnp.int32, values[0].shape, axis)
    for place, bit in enumerate(reversed(bits)):
        step, span = 1 << place, 1 << bit
        keep = (index & span) == 0
        for i in range(len(values)):
            if i & step:
                continue
            a, b = values[i], values[i + step]
            values[i] = jnp.where(keep, a, pltpu.roll(b, span, axis))
            values[i + step] = jnp.where(keep, pltpu.roll(a, size - span, axis), b)
    return values


def halves(values):
    high = values.astype(BF16)
    return high, (values - high.astype(F32)).astype(BF16)


def matmul(a, b):
    return lax.dot_general(a, b, (((1,), (0,)), ((), ())), preferred_element_type=F32)


def exact_matmul(a, b):
    return lax.dot_general(
        a,
        b,
        (((1,), (0,)), ((), ())),
        precision=lax.Precision.HIGHEST,
        preferred_element_type=F32,
    )


def transform(values, table):
    high, low = halves(values)
    return matmul(high, table[0]) + matmul(low, table[0]) + matmul(high, table[1])


def call(kernel, out_shapes, *args, scratch=(), flops=1000000):
    shapes = [jax.ShapeDtypeStruct(s, F32) for s in out_shapes]
    return pl.pallas_call(
        kernel,
        out_shape=shapes if len(shapes) > 1 else shapes[0],
        scratch_shapes=list(scratch),
        compiler_params=pltpu.CompilerParams(vmem_limit_bytes=VMEM_BYTES),
        cost_estimate=pl.CostEstimate(flops=flops, bytes_accessed=400000, transcendentals=0),
    )(*args)


def group_of(place_ref, m):
    return (place_ref[0] - m) & 3


def down_columns(place_ref, down_ref):
    down = down_ref[...]
    lane = lax.broadcasted_iota(jnp.int32, down.shape, 1)
    columns = []
    for m in range(GROUPS):
        for i in range(2):
            pick = jnp.where(lane == 2 * group_of(place_ref, m) + i, down, 0.0)
            column = jnp.sum(pick, axis=1, keepdims=True)
            columns.append(jnp.broadcast_to(column, (Q_DEV, LANES)))
    return columns


def lowered(kept, rows, columns):
    total = kept
    for g in range(GROUPS):
        for i in range(2):
            total = total - columns[2 * g + i] * rows(g, i)
    return total


def spread_rows(piece, out_ref):
    for h in range(2):
        parts = [piece(p, r * SIDE + h * LANES) for p in range(2) for r in range(8)]
        for c, part in enumerate(exchange(parts, (6, 5, 4, 3))):
            out_ref[h * 16 + c] = part


def rows_kernel(x_ref, out_ref):
    spread_rows(lambda p, at: x_ref[0, :, p, at : at + LANES], out_ref)


def column_transform(in_ref, table_ref, hold_ref):
    hold_ref[...] = jnp.zeros_like(hold_ref)
    for h in range(2):
        parts = exchange([in_ref[h * 16 + s] for s in range(16)], (6, 2, 1, 0))
        for i, part in enumerate(parts):
            hold_ref[i, 0:Q_DEV, h * LANES : (h + 1) * LANES] = part
    result = transform(hold_ref[...].reshape(128, SIDE), table_ref)
    return result.reshape(16, 8, SIDE)


def columns_kernel(in_ref, table_ref, out_ref, hold_ref):
    result = column_transform(in_ref, table_ref, hold_ref)
    lane = lax.broadcasted_iota(jnp.int32, (8, LANES), 1)
    first = (lane & 8) == 0
    for p in range(2):
        pairs = []
        for h in range(2):
            parts = [result[p * 8 + k][:, h * LANES : (h + 1) * LANES] for k in range(8)]
            pairs += exchange(parts, (6, 5, 4))
        for i in range(16):
            out_ref[2 * i + 1, p] = pairs[i][:Q_DEV]
            both = jnp.where(
                first, pltpu.roll(pairs[i - 1], LANES - 8, 1), pltpu.roll(pairs[i], 8, 1)
            )
            out_ref[2 * i, p] = both[:Q_DEV]


def evals_kernel(in_ref, table_ref, e0_ref, e1_ref, hold_ref):
    hold_ref[...] = jnp.zeros_like(hold_ref)
    for p in range(2):
        for h in range(2):
            parts = exchange([in_ref[h * 16 + c, p] for c in range(16)], (3, 2, 1, 0))
            for row, part in enumerate(parts):
                hold_ref[p * 16 + row, 0:Q_DEV, h * LANES : (h + 1) * LANES] = part
    result = transform(hold_ref[...].reshape(256, SIDE), table_ref).reshape(32, 8, SIDE)
    for row in range(16):
        at = slice(row * SIDE, (row + 1) * SIDE)
        e0_ref[:, at] = result[row][:Q_DEV]
        e1_ref[:, at] = result[16 + row][:Q_DEV]


def products_kernel(
    place_ref, e1a_ref, e1b_ref, e1c_ref, e1d_ref, up_ref, keys_ref,
    kept_ref, spare0_ref, spare1_ref, raised_ref, stage_ref,
):
    step = pl.program_id(0)

    @pl.when(step == 0)
    def _():
        iota = lambda shape, axis: lax.broadcasted_iota(jnp.int32, shape, axis)

        def limb(q):
            group = group_of(place_ref, q >> 3)
            return jnp.where((q & 7) < Q_DEV, 6 * group + (q & 7), -1)

        pick = (iota((24, 32), 0) == limb(iota((24, 32), 1))).astype(F32)
        spread = exact_matmul(up_ref[...], pick)
        digit = limb(iota((8, 32), 1)) >> 3
        factors = jnp.concatenate(
            [jnp.where(digit == d, spread, 0.0) for d in range(DNUM)], axis=0
        )
        fh, fl = halves(factors)
        lhs = jnp.concatenate([fh, fh, fl], axis=1)
        stage_ref[...] = jnp.zeros_like(stage_ref)
        for m, ref in enumerate((e1a_ref, e1b_ref, e1c_ref, e1d_ref)):
            stage_ref[8 * m : 8 * m + Q_DEV, :] = ref[...]
        for part in range(8):
            at = slice(part * 512, (part + 1) * 512)
            eh, el = halves(stage_ref[:, at])
            raised_ref[:, at] = matmul(lhs, jnp.concatenate([eh, el, eh], axis=0))

    spares = (spare0_ref, spare1_ref)

    def body(t, carry):
        base = pl.multiple_of(step * CHUNK + t * LANES, LANES)
        here = pl.ds(pl.multiple_of(t * LANES, LANES), LANES)
        for k in range(1, BABY):
            at = pl.ds(base + (8 - k) * SIDE, LANES)
            views = [raised_ref[d * 8 : d * 8 + 8, at] for d in range(DNUM)]
            for s in range(2):
                total = None
                for d in range(DNUM):
                    term = views[d] * keys_ref[k - 1, d, s, :, here].astype(F32)
                    total = term if total is None else total + term
                kept_ref[s, k - 1, :, here] = total
                spares[s][2 * k - 2 : 2 * k, here] = total[Q_DEV:]
        return carry

    lax.fori_loop(0, CHUNK // LANES, body, 0)


def babies_kernel(
    poly, place_ref, kept_ref, spare0_ref, spare1_ref, spare2_ref, spare3_ref,
    evals_ref, down_ref, diag_ref, *out_refs,
):
    step = pl.program_id(0)
    columns = down_columns(place_ref, down_ref)
    spares = (spare0_ref, spare1_ref, spare2_ref, spare3_ref)

    def body(t, carry):
        base = pl.multiple_of(step * CHUNK + t * LANES, LANES)
        here = pl.ds(pl.multiple_of(t * LANES, LANES), LANES)
        babies = [evals_ref[:, pl.ds(base + POINTS_DEV, LANES)]]
        for k in range(1, BABY):
            rows = lambda m, i: spares[m][2 * k - 2 + i : 2 * k - 1 + i, here]
            baby = lowered(kept_ref[0, k - 1, 0:Q_DEV, here], rows, columns)
            if poly == 0:
                baby = baby + evals_ref[:, pl.ds(base + (8 - k) * SIDE, LANES)]
            babies.append(baby)
        for j in range(GIANT):
            inner = None
            for k in range(BABY):
                term = diag_ref[j, k, :, here].astype(F32) * babies[k]
                inner = term if inner is None else inner + term
            if poly == 0:
                at = 6 * (j % 4)
                out_refs[j // 4][at : at + 6, here] = inner
            elif j % 4 == 0:
                out_refs[3 + j // 4][:, here] = inner
            else:
                at = 6 * (j // 4)
                out_refs[j % 4 - 1][at : at + 6, here] = inner
        return carry

    lax.fori_loop(0, CHUNK // LANES, body, 0)


def whole(a):
    return pl.BlockSpec(a.shape, lambda i, n=a.ndim: (0,) * n)


def lanes(*lead):
    return pl.BlockSpec(lead + (CHUNK,), lambda i, n=len(lead): (0,) * n + (i,))


PLACE = pl.BlockSpec(memory_space=pltpu.SMEM)


def products_call(place, evals, up, keys):
    return pl.pallas_call(
        products_kernel,
        grid=(POINTS_DEV // CHUNK,),
        in_specs=[PLACE] + [whole(e) for e in evals] + [whole(up), lanes(7, 3, 2, 8)],
        out_specs=[lanes(2, 7, 8), lanes(14), lanes(14)],
        out_shape=[
            jax.ShapeDtypeStruct((2, 7, 8, POINTS_DEV), F32),
            jax.ShapeDtypeStruct((14, POINTS_DEV), F32),
            jax.ShapeDtypeStruct((14, POINTS_DEV), F32),
        ],
        scratch_shapes=[pltpu.VMEM((24, HALO), F32), pltpu.VMEM((32, HALO), F32)],
        compiler_params=pltpu.CompilerParams(vmem_limit_bytes=VMEM_BYTES),
        cost_estimate=pl.CostEstimate(flops=40000000, bytes_accessed=4000000, transcendentals=0),
    )(place, *evals, up, keys)


def babies_call(poly, place, kept, spares, evals, down, diagonals):
    rows = (24, 24) if poly == 0 else (12, 12, 12, 6, 6)
    part = pl.BlockSpec((1, 7, 8, CHUNK), lambda i: (poly, 0, 0, i))
    return pl.pallas_call(
        functools.partial(babies_kernel, poly),
        grid=(POINTS_DEV // CHUNK,),
        in_specs=[PLACE, part]
        + [lanes(14)] * 4
        + [whole(evals), whole(down), lanes(8, 8, Q_DEV)],
        out_specs=[lanes(r) for r in rows],
        out_shape=[jax.ShapeDtypeStruct((r, POINTS_DEV), F32) for r in rows],
        compiler_params=pltpu.CompilerParams(vmem_limit_bytes=VMEM_BYTES),
        cost_estimate=pl.CostEstimate(flops=40000000, bytes_accessed=6000000, transcendentals=0),
    )(place, kept, *spares, evals, down, diagonals)


def sort_kernel(got1_ref, got2_ref, got3_ref, four_ref, near_ref, far_ref):
    far_ref[0:6, :] = four_ref[...]
    for r, got in enumerate((got1_ref, got2_ref, got3_ref)):
        near_ref[6 * r : 6 * r + 6, :] = got[0:6, :]
        far_ref[6 + 6 * r : 12 + 6 * r, :] = got[6:12, :]
    near_ref[18:24, :] = jnp.zeros((6, POINTS_DEV), F32)


def pair_sum_kernel(low_ref, high_ref, *out_refs):
    for r, out_ref in enumerate(out_refs):
        at = slice(6 * r, 6 * r + 6)
        out_ref[...] = low_ref[at, :] + high_ref[at, :]


def giants_kernel(
    first, place_ref, part0_ref, part1_ref, part2_ref, part3_ref, up_ref, keys_ref, *refs
):
    before_ref = spare_ref = None
    if first == 1:
        total_ref, raised_ref, factor_ref = refs
    else:
        before_ref, total_ref, spare_ref, raised_ref, factor_ref = refs
    step = pl.program_id(0)

    @pl.when(step == 0)
    def _():
        iota = lambda shape, axis: lax.broadcasted_iota(jnp.int32, shape, axis)

        def source(q):
            block = (q >= 24).astype(jnp.int32) + (q >= 48) + (q >= 72)
            rest = q - 24 * block
            giant = (rest * 43) >> 8
            return giant, 6 * group_of(place_ref, block) + rest - 6 * giant

        pick = (iota((24, 96), 0) == source(iota((24, 96), 1))[1]).astype(F32)
        spread = exact_matmul(up_ref[...], pick)
        held, limb = source(iota((8, 96), 1))
        for j in range(4):
            parts = [
                jnp.where((held == j) & ((limb >> 3) == d), spread, 0.0) for d in range(DNUM)
            ]
            at = slice(j * 24, j * 24 + 24)
            fh, fl = halves(jnp.concatenate(parts, axis=0))
            factor_ref[0, at], factor_ref[1, at] = fh.astype(F32), fl.astype(F32)

    fh, fl = factor_ref[0].astype(BF16), factor_ref[1].astype(BF16)
    parts = (part0_ref, part1_ref, part2_ref, part3_ref)
    eh, el = halves(jnp.concatenate([ref[...] for ref in parts], axis=0))
    raised_ref[...] = matmul(fh, eh) + matmul(fh, el) + matmul(fl, eh)

    def body(t, carry):
        here = pl.ds(pl.multiple_of(t * LANES, LANES), LANES)
        sums = [None, None]
        if before_ref is not None:
            sums = [before_ref[s, :, here] for s in range(2)]
        for j in range(3 if first == 1 else 4):
            for d in range(DNUM):
                at = j * 24 + d * 8
                value = raised_ref[at : at + 8, here]
                for s in range(2):
                    key = keys_ref[first - 1 + j, d, s, :, here].astype(F32)
                    sums[s] = value * key if sums[s] is None else sums[s] + value * key
        if before_ref is None:
            total_ref[0, :, here], total_ref[1, :, here] = sums
        else:
            for s in range(2):
                total_ref[s, :, here] = sums[s][:Q_DEV]
                spare_ref[2 * s : 2 * s + 2, here] = sums[s][Q_DEV:]
        return carry

    lax.fori_loop(0, CHUNK // LANES, body, 0)


def giants_call(first, place, parts, up, keys, before=None):
    more = [] if before is None else [before]
    shapes = [(2, 8)] if before is None else [(2, Q_DEV), (4,)]
    return pl.pallas_call(
        functools.partial(giants_kernel, first),
        grid=(POINTS_DEV // CHUNK,),
        in_specs=[PLACE]
        + [lanes(24)] * 4
        + [whole(up), lanes(7, 3, 2, 8)]
        + [lanes(2, 8) for _ in more],
        out_specs=[lanes(*shape) for shape in shapes],
        out_shape=[jax.ShapeDtypeStruct(shape + (POINTS_DEV,), F32) for shape in shapes],
        scratch_shapes=[pltpu.VMEM((96, CHUNK), F32), pltpu.VMEM((2, 96, 96), F32)],
        compiler_params=pltpu.CompilerParams(vmem_limit_bytes=VMEM_BYTES),
        cost_estimate=pl.CostEstimate(flops=20000000, bytes_accessed=2000000, transcendentals=0),
    )(place, *parts, up, keys, *more)


def lower_kernel(
    place_ref, total_ref, spare0_ref, spare1_ref, spare2_ref, spare3_ref, down_ref,
    zero_ref, rest0_ref, rest1_ref, rest2_ref, rest3_ref, out_ref,
):
    columns = down_columns(place_ref, down_ref)
    spares = (spare0_ref, spare1_ref, spare2_ref, spare3_ref)

    def piece(p, at):
        here = slice(at, at + LANES)
        rows = lambda m, i: spares[m][2 * p + i : 2 * p + i + 1, here]
        value = total_ref[p, :, here]
        if p == 0:
            for rest in (rest0_ref, rest1_ref, rest2_ref, rest3_ref):
                value = value + rest[:, here]
        else:
            value = value + zero_ref[:, here]
        return lowered(value, rows, columns)

    spread_rows(piece, out_ref)


def lower_call(place, total, spares, down, zero, rests):
    out = (SLOTS, Q_DEV, LANES)
    return pl.pallas_call(
        lower_kernel,
        in_specs=[PLACE] + [pl.BlockSpec(memory_space=pltpu.VMEM)] * 11,
        out_specs=pl.BlockSpec(memory_space=pltpu.VMEM),
        out_shape=jax.ShapeDtypeStruct(out, F32),
        compiler_params=pltpu.CompilerParams(vmem_limit_bytes=VMEM_BYTES),
        cost_estimate=pl.CostEstimate(flops=1000000, bytes_accessed=400000, transcendentals=0),
    )(place, total, *spares, down, zero, *rests)


def inverse_columns_kernel(in_ref, table_ref, out_ref, hold_ref):
    result = column_transform(in_ref, table_ref, hold_ref)
    for h in range(2):
        parts = [result[i][:, h * LANES : (h + 1) * LANES] for i in range(16)]
        for g, part in enumerate(exchange(parts, (6, 5, 4, 3))):
            out_ref[h * 16 + g] = part[:Q_DEV]


def inverse_rows_kernel(in_ref, table_ref, out_ref, hold_ref):
    hold_ref[...] = jnp.zeros_like(hold_ref)
    for h in range(2):
        parts = exchange([in_ref[h * 16 + c] for c in range(16)], (6, 2, 1, 0))
        for i, part in enumerate(parts):
            hold_ref[i, 0:Q_DEV, h * LANES : (h + 1) * LANES] = part
    result = transform(hold_ref[...].reshape(128, SIDE), table_ref).reshape(16, 8, SIDE)
    for p in range(2):
        for r in range(8):
            out_ref[0, :, p, r * SIDE : (r + 1) * SIDE] = result[p * 8 + r][:Q_DEV]


def swap(values, axis):
    return lax.all_to_all(values, axis, split_axis=0, concat_axis=0, tiled=True)


def shifted(block, distance):
    route = [(i, (i + distance) % SLOTS) for i in range(SLOTS)]
    return lax.ppermute(block, "slot", route)


def forward(ciphertexts):
    col_fwd, row_fwd, _, _ = dct_constants()
    hold = [pltpu.VMEM((16, 8, SIDE), F32)]
    parts = jnp.transpose(ciphertexts, (0, 2, 1, 3))
    sent = call(rows_kernel, [(SLOTS, Q_DEV, LANES)], parts)
    held = swap(sent, "slot")
    sent = call(
        columns_kernel, [(SLOTS, 2, Q_DEV, LANES)], held, col_fwd, scratch=hold, flops=50000000
    )
    held = swap(sent, "slot")
    return call(
        evals_kernel,
        [(Q_DEV, HALO), (Q_DEV, HALO)],
        held,
        row_fwd,
        scratch=[pltpu.VMEM((32, 8, SIDE), F32)],
        flops=100000000,
    )


def inverse(sent):
    _, _, col_inv, row_inv = dct_constants()
    hold = [pltpu.VMEM((16, 8, SIDE), F32)]
    held = swap(sent, "slot")
    sent = call(
        inverse_columns_kernel,
        [(SLOTS, Q_DEV, LANES)],
        held,
        col_inv,
        scratch=hold,
        flops=50000000,
    )
    held = swap(sent, "slot")
    out = call(
        inverse_rows_kernel,
        [(1, Q_DEV, 2, POINTS_DEV)],
        held,
        row_inv,
        scratch=hold,
        flops=50000000,
    )
    return jnp.transpose(out, (0, 2, 1, 3))


def gathered(block):
    routes = [[(i, (i + m) % GROUPS) for i in range(GROUPS)] for m in range(GROUPS)]
    return [block] + [lax.ppermute(block, "limb", routes[m]) for m in range(1, GROUPS)]


def after(values, others):
    return lax.optimization_barrier((*values, *others))[: len(values)]


def together(*groups):
    flat = lax.optimization_barrier([value for group in groups for value in group])
    return [[flat.pop(0) for _ in group] for group in groups]


def per_device(ciphertexts, diagonals, baby_keys, giant_keys, up, down):
    place = lax.axis_index("limb").astype(jnp.int32).reshape(1)
    e0, e1 = forward(ciphertexts)
    kept, spare0, spare1 = products_call(place, gathered(e1), up, baby_keys)
    *sends, zero, four = babies_call(1, place, kept, gathered(spare1), e1, down, diagonals)
    spares0 = gathered(spare0)
    gots = [shifted(send, r + 1) for r, send in enumerate(sends)]
    gots, spares0 = together(gots, spares0)
    low, high = babies_call(0, place, kept, spares0, e0, down, diagonals)
    near, far = call(sort_kernel, [(24, POINTS_DEV)] * 2, *gots, four, flops=10000)
    far = shifted(far, 4)
    high = shifted(high, 4)
    nears = gathered(near)
    (before,) = giants_call(1, place, nears, up, giant_keys)
    (high,), (before,) = together([high], [before])
    rests = call(pair_sum_kernel, [(Q_DEV, POINTS_DEV)] * 4, low, high, flops=10000)
    rests = [rests[0]] + [shifted(rests[r], r) for r in range(1, 4)]
    total, spare = giants_call(4, place, gathered(far), up, giant_keys, before)
    return inverse(lower_call(place, total, gathered(spare), down, zero, rests))


def solution(mesh):
    placed = (
        P("ct", None, "limb", "slot"),
        P(None, None, "limb", "slot"),
        P(None, None, None, "limb", "slot"),
        P(None, None, None, "limb", "slot"),
        P("limb", None),
        P("limb", None),
    )
    return jax.shard_map(
        per_device,
        mesh=mesh,
        in_specs=placed,
        out_specs=P("ct", None, "limb", "slot"),
        check_vma=False,
    )
```

```python
import functools

import numpy as np
import jax
import jax.numpy as jnp
import ml_dtypes
from jax import lax
from jax.experimental import pallas as pl
from jax.experimental.pallas import tpu as pltpu
from jax.sharding import PartitionSpec as P

SIDE = 256
DNUM = 3
BABY = 8
GIANT = 8
Q_DEV = 6
LANES = 128
POINTS_DEV = 2048
HALO = 2 * POINTS_DEV
SLOTS = 32
GROUPS = 4
CHUNK = 1024
VMEM_BYTES = 14 * 1024 * 1024
F32 = jnp.float32
BF16 = jnp.bfloat16


def split_constant(values):
    high = values.astype(ml_dtypes.bfloat16)
    low = (values - high.astype(np.float64)).astype(ml_dtypes.bfloat16)
    return np.stack([high, low])


def cosine_matrix():
    k = np.arange(SIDE, dtype=np.float64)[:, None]
    n = np.arange(SIDE, dtype=np.float64)[None, :]
    scale = np.where(k == 0, np.sqrt(1.0 / SIDE), np.sqrt(2.0 / SIDE))
    return scale * np.cos(np.pi * (n + 0.5) * k / SIDE)


def lane_orders():
    lane = np.arange(SIDE)
    half, low = lane // LANES, lane % LANES
    block, rest = low // 64, low % 64
    rows = half * 128 + block * 64 + (rest % 8) * 8 + rest // 8
    cols_fwd = half * 128 + (low % 16) * 8 + low // 16
    c = (low // 64) * 8 + low % 8
    k = (low // 8) % 8
    cols_inv = half * 128 + c * 8 + k
    return rows, cols_fwd, cols_inv


def dct_constants():
    c = cosine_matrix()
    rows, cols_fwd, cols_inv = lane_orders()
    return (
        split_constant(c.T[rows]),
        split_constant(c.T[cols_fwd]),
        split_constant(c[rows]),
        split_constant(c[cols_inv]),
    )


def exchange(values, bits, axis=1):
    values = list(values)
    size = values[0].shape[axis]
    index = lax.broadcasted_iota(jnp.int32, values[0].shape, axis)
    for place, bit in enumerate(reversed(bits)):
        step, span = 1 << place, 1 << bit
        keep = (index & span) == 0
        for i in range(len(values)):
            if i & step:
                continue
            a, b = values[i], values[i + step]
            values[i] = jnp.where(keep, a, pltpu.roll(b, span, axis))
            values[i + step] = jnp.where(keep, pltpu.roll(a, size - span, axis), b)
    return values


def halves(values):
    high = values.astype(BF16)
    return high, (values - high.astype(F32)).astype(BF16)


def matmul(a, b):
    return lax.dot_general(a, b, (((1,), (0,)), ((), ())), preferred_element_type=F32)


def exact_matmul(a, b):
    return lax.dot_general(
        a,
        b,
        (((1,), (0,)), ((), ())),
        precision=lax.Precision.HIGHEST,
        preferred_element_type=F32,
    )


def transform(values, table):
    high, low = halves(values)
    return matmul(high, table[0]) + matmul(low, table[0]) + matmul(high, table[1])


def call(kernel, out_shapes, *args, scratch=(), flops=1000000):
    shapes = [jax.ShapeDtypeStruct(s, F32) for s in out_shapes]
    return pl.pallas_call(
        kernel,
        out_shape=shapes if len(shapes) > 1 else shapes[0],
        scratch_shapes=list(scratch),
        compiler_params=pltpu.CompilerParams(vmem_limit_bytes=VMEM_BYTES),
        cost_estimate=pl.CostEstimate(flops=flops, bytes_accessed=400000, transcendentals=0),
    )(*args)


def group_of(place_ref, m):
    return (place_ref[0] - m) & 3


def down_columns(place_ref, down_ref):
    down = down_ref[...]
    lane = lax.broadcasted_iota(jnp.int32, down.shape, 1)
    columns = []
    for m in range(GROUPS):
        for i in range(2):
            pick = jnp.where(lane == 2 * group_of(place_ref, m) + i, down, 0.0)
            column = jnp.sum(pick, axis=1, keepdims=True)
            columns.append(jnp.broadcast_to(column, (Q_DEV, LANES)))
    return columns


def lowered(kept, rows, columns):
    total = kept
    for g in range(GROUPS):
        for i in range(2):
            total = total - columns[2 * g + i] * rows(g, i)
    return total


def spread_rows(piece, out_ref):
    for h in range(2):
        parts = [piece(p, r * SIDE + h * LANES) for p in range(2) for r in range(8)]
        for c, part in enumerate(exchange(parts, (6, 5, 4, 3))):
            out_ref[h * 16 + c] = part


def rows_kernel(x_ref, out_ref):
    spread_rows(lambda p, at: x_ref[0, :, p, at : at + LANES], out_ref)


def column_transform(in_ref, table_ref, hold_ref):
    hold_ref[...] = jnp.zeros_like(hold_ref)
    for h in range(2):
        parts = exchange([in_ref[h * 16 + s] for s in range(16)], (6, 2, 1, 0))
        for i, part in enumerate(parts):
            hold_ref[i, 0:Q_DEV, h * LANES : (h + 1) * LANES] = part
    result = transform(hold_ref[...].reshape(128, SIDE), table_ref)
    return result.reshape(16, 8, SIDE)


def columns_kernel(in_ref, table_ref, out_ref, hold_ref):
    result = column_transform(in_ref, table_ref, hold_ref)
    lane = lax.broadcasted_iota(jnp.int32, (8, LANES), 1)
    first = (lane & 8) == 0
    for p in range(2):
        pairs = []
        for h in range(2):
            parts = [result[p * 8 + k][:, h * LANES : (h + 1) * LANES] for k in range(8)]
            pairs += exchange(parts, (6, 5, 4))
        for i in range(16):
            out_ref[2 * i + 1, p] = pairs[i][:Q_DEV]
            both = jnp.where(
                first, pltpu.roll(pairs[i - 1], LANES - 8, 1), pltpu.roll(pairs[i], 8, 1)
            )
            out_ref[2 * i, p] = both[:Q_DEV]


def evals_kernel(in_ref, table_ref, e0_ref, e1_ref, sent_ref, hold_ref):
    hold_ref[...] = jnp.zeros_like(hold_ref)
    for p in range(2):
        for h in range(2):
            parts = exchange([in_ref[h * 16 + c, p] for c in range(16)], (3, 2, 1, 0))
            for row, part in enumerate(parts):
                hold_ref[p * 16 + row, 0:Q_DEV, h * LANES : (h + 1) * LANES] = part
    result = transform(hold_ref[...].reshape(256, SIDE), table_ref).reshape(32, 8, SIDE)
    for row in range(16):
        at = slice(row * SIDE, (row + 1) * SIDE)
        e0_ref[:, at] = result[row][:Q_DEV]
        e1_ref[:, at] = result[16 + row][:Q_DEV]
        for i in range(3):
            sent_ref[i, :, at] = result[16 + row][2 * i : 2 * i + 2]


def factors_kernel(place_ref, up_ref, baby_ref, giant_ref):
    iota = lambda shape, axis: lax.broadcasted_iota(jnp.int32, shape, axis)
    up = up_ref[...]

    def spread(held, limb, columns):
        pick = (iota((24, columns), 0) == limb).astype(F32)
        wide = exact_matmul(up, pick)
        digit = limb[0:8] >> 3
        return [jnp.where(held[0:8] & (digit == d), wide, 0.0) for d in range(DNUM)]

    q = iota((24, 32), 1)
    used = (q & 7) < Q_DEV
    limb = jnp.where(used, 6 * group_of(place_ref, q >> 3) + (q & 7), -8)
    fh, fl = halves(jnp.concatenate(spread(used, limb, 32), axis=0))
    baby_ref[...] = jnp.concatenate([fh, fh, fl], axis=1).astype(F32)
    q = iota((24, 96), 1)
    block = (q >= 24).astype(jnp.int32) + (q >= 48) + (q >= 72)
    rest = q - 24 * block
    giant = (rest * 43) >> 8
    limb = 6 * group_of(place_ref, block) + rest - 6 * giant
    for j in range(4):
        at = slice(j * 24, j * 24 + 24)
        fh, fl = halves(jnp.concatenate(spread(giant == j, limb, 96), axis=0))
        giant_ref[0, at], giant_ref[1, at] = fh.astype(F32), fl.astype(F32)


def factors_call(place, up):
    return pl.pallas_call(
        factors_kernel,
        in_specs=[pl.BlockSpec(memory_space=pltpu.SMEM), pl.BlockSpec(memory_space=pltpu.VMEM)],
        out_specs=[pl.BlockSpec(memory_space=pltpu.VMEM)] * 2,
        out_shape=[
            jax.ShapeDtypeStruct((24, 96), F32),
            jax.ShapeDtypeStruct((2, 96, 96), F32),
        ],
        compiler_params=pltpu.CompilerParams(vmem_limit_bytes=VMEM_BYTES),
        cost_estimate=pl.CostEstimate(flops=1000000, bytes_accessed=100000, transcendentals=0),
    )(place, up)


def products_kernel(
    e1a_ref, e1b_ref, e1c_ref, e1d_ref, factors_ref, keys_ref,
    kept_ref, spare0_ref, spare1_ref, raised_ref, stage_ref,
):
    step = pl.program_id(0)

    @pl.when(step == 0)
    def _():
        lhs = factors_ref[...].astype(BF16)
        stage_ref[...] = jnp.zeros_like(stage_ref)
        stage_ref[0:Q_DEV, :] = e1a_ref[...]
        for m, ref in enumerate((e1b_ref, e1c_ref, e1d_ref), 1):
            for i in range(3):
                stage_ref[8 * m + 2 * i : 8 * m + 2 * i + 2, :] = ref[i]
        for part in range(8):
            at = slice(part * 512, (part + 1) * 512)
            eh, el = halves(stage_ref[:, at])
            raised_ref[:, at] = matmul(lhs, jnp.concatenate([eh, el, eh], axis=0))

    spares = (spare0_ref, spare1_ref)

    def body(t, carry):
        base = pl.multiple_of(step * CHUNK + t * LANES, LANES)
        here = pl.ds(pl.multiple_of(t * LANES, LANES), LANES)
        for k in range(1, BABY):
            at = pl.ds(base + (8 - k) * SIDE, LANES)
            views = [raised_ref[d * 8 : d * 8 + 8, at] for d in range(DNUM)]
            for s in range(2):
                total = None
                for d in range(DNUM):
                    term = views[d] * keys_ref[k - 1, d, s, :, here].astype(F32)
                    total = term if total is None else total + term
                kept_ref[s, k - 1, :, here] = total
                spares[s][k - 1, :, here] = total[Q_DEV:]
        return carry

    lax.fori_loop(0, CHUNK // LANES, body, 0)


def babies_kernel(
    poly, place_ref, kept_ref, spare0_ref, spare1_ref, spare2_ref, spare3_ref,
    evals_ref, down_ref, diag_ref, *out_refs,
):
    step = pl.program_id(0)
    columns = down_columns(place_ref, down_ref)
    spares = (spare0_ref, spare1_ref, spare2_ref, spare3_ref)

    def body(t, carry):
        base = pl.multiple_of(step * CHUNK + t * LANES, LANES)
        here = pl.ds(pl.multiple_of(t * LANES, LANES), LANES)
        babies = [evals_ref[:, pl.ds(base + POINTS_DEV, LANES)]]
        for k in range(1, BABY):
            rows = lambda m, i: spares[m][k - 1, i : i + 1, here]
            baby = lowered(kept_ref[0, k - 1, 0:Q_DEV, here], rows, columns)
            if poly == 0:
                baby = baby + evals_ref[:, pl.ds(base + (8 - k) * SIDE, LANES)]
            babies.append(baby)
        for j in range(GIANT):
            inner = None
            for k in range(BABY):
                term = diag_ref[j, k, :, here].astype(F32) * babies[k]
                inner = term if inner is None else inner + term
            if poly == 0:
                at = 6 * (j % 4)
                out_refs[j // 4][at : at + 6, here] = inner
            elif j % 4 == 0:
                out_refs[3 + j // 4][:, here] = inner
            else:
                for i in range(3):
                    out_refs[j % 4 - 1][3 * (j // 4) + i, :, here] = inner[2 * i : 2 * i + 2]
        return carry

    lax.fori_loop(0, CHUNK // LANES, body, 0)


def whole(a):
    return pl.BlockSpec(a.shape, lambda i, n=a.ndim: (0,) * n)


def lanes(*lead):
    return pl.BlockSpec(lead + (CHUNK,), lambda i, n=len(lead): (0,) * n + (i,))


PLACE = pl.BlockSpec(memory_space=pltpu.SMEM)


def products_call(evals, factors, keys):
    return pl.pallas_call(
        products_kernel,
        grid=(POINTS_DEV // CHUNK,),
        in_specs=[whole(e) for e in evals] + [whole(factors), lanes(7, 3, 2, 8)],
        out_specs=[lanes(2, 7, 8), lanes(7, 2), lanes(7, 2)],
        out_shape=[
            jax.ShapeDtypeStruct((2, 7, 8, POINTS_DEV), F32),
            jax.ShapeDtypeStruct((7, 2, POINTS_DEV), F32),
            jax.ShapeDtypeStruct((7, 2, POINTS_DEV), F32),
        ],
        scratch_shapes=[pltpu.VMEM((24, HALO), F32), pltpu.VMEM((32, HALO), F32)],
        compiler_params=pltpu.CompilerParams(vmem_limit_bytes=VMEM_BYTES),
        cost_estimate=pl.CostEstimate(flops=40000000, bytes_accessed=4000000, transcendentals=0),
    )(*evals, factors, keys)


def babies_call(poly, place, kept, spares, evals, down, diagonals):
    rows = [(24,), (24,)] if poly == 0 else [(6, 2)] * 3 + [(6,)] * 2
    part = pl.BlockSpec((1, 7, 8, CHUNK), lambda i: (poly, 0, 0, i))
    return pl.pallas_call(
        functools.partial(babies_kernel, poly),
        grid=(POINTS_DEV // CHUNK,),
        in_specs=[PLACE, part]
        + [lanes(7, 2)] * 4
        + [whole(evals), whole(down), lanes(8, 8, Q_DEV)],
        out_specs=[lanes(*r) for r in rows],
        out_shape=[jax.ShapeDtypeStruct((*r, POINTS_DEV), F32) for r in rows],
        compiler_params=pltpu.CompilerParams(vmem_limit_bytes=VMEM_BYTES),
        cost_estimate=pl.CostEstimate(flops=40000000, bytes_accessed=6000000, transcendentals=0),
    )(place, kept, *spares, evals, down, diagonals)


def sort_kernel(got1_ref, got2_ref, got3_ref, four_ref, near_ref, far_ref):
    far_ref[0:6, :] = four_ref[...]
    for r, got in enumerate((got1_ref, got2_ref, got3_ref)):
        for i in range(3):
            near_ref[3 * r + i] = got[i]
            far_ref[6 + 6 * r + 2 * i : 8 + 6 * r + 2 * i, :] = got[3 + i]


def pair_sum_kernel(low_ref, high_ref, *out_refs):
    for r, out_ref in enumerate(out_refs):
        at = slice(6 * r, 6 * r + 6)
        out_ref[...] = low_ref[at, :] + high_ref[at, :]


def giants_kernel(
    first, part0_ref, part1_ref, part2_ref, part3_ref, factor_ref, keys_ref, *refs
):
    before_ref = spare_ref = None
    if first == 1:
        total_ref, raised_ref, stage_ref = refs
    else:
        before_ref, total_ref, spare_ref, raised_ref = refs
    fh, fl = factor_ref[0].astype(BF16), factor_ref[1].astype(BF16)
    parts = (part0_ref, part1_ref, part2_ref, part3_ref)
    if first == 1:
        for m, ref in enumerate(parts):
            for i in range(9):
                stage_ref[24 * m + 2 * i : 24 * m + 2 * i + 2, :] = ref[i]
            stage_ref[24 * m + 18 : 24 * m + 24, :] = jnp.zeros((6, CHUNK), F32)
        held = stage_ref[...]
    else:
        held = jnp.concatenate([ref[...] for ref in parts], axis=0)
    eh, el = halves(held)
    raised_ref[...] = matmul(fh, eh) + matmul(fh, el) + matmul(fl, eh)

    def body(t, carry):
        here = pl.ds(pl.multiple_of(t * LANES, LANES), LANES)
        sums = [None, None]
        if before_ref is not None:
            sums = [before_ref[s, :, here] for s in range(2)]
        for j in range(3 if first == 1 else 4):
            for d in range(DNUM):
                at = j * 24 + d * 8
                value = raised_ref[at : at + 8, here]
                for s in range(2):
                    key = keys_ref[first - 1 + j, d, s, :, here].astype(F32)
                    sums[s] = value * key if sums[s] is None else sums[s] + value * key
        if before_ref is None:
            total_ref[0, :, here], total_ref[1, :, here] = sums
        else:
            for s in range(2):
                total_ref[s, :, here] = sums[s][:Q_DEV]
                spare_ref[2 * s : 2 * s + 2, here] = sums[s][Q_DEV:]
        return carry

    lax.fori_loop(0, CHUNK // LANES, body, 0)


def giants_call(first, parts, factors, keys, before=None):
    more = [] if before is None else [before]
    shapes = [(2, 8)] if before is None else [(2, Q_DEV), (4,)]
    return pl.pallas_call(
        functools.partial(giants_kernel, first),
        grid=(POINTS_DEV // CHUNK,),
        in_specs=[lanes(9, 2) if first == 1 else lanes(24)] * 4
        + [whole(factors), lanes(7, 3, 2, 8)]
        + [lanes(2, 8) for _ in more],
        out_specs=[lanes(*shape) for shape in shapes],
        out_shape=[jax.ShapeDtypeStruct(shape + (POINTS_DEV,), F32) for shape in shapes],
        scratch_shapes=[pltpu.VMEM((96, CHUNK), F32)] * (2 if first == 1 else 1),
        compiler_params=pltpu.CompilerParams(vmem_limit_bytes=VMEM_BYTES),
        cost_estimate=pl.CostEstimate(flops=20000000, bytes_accessed=2000000, transcendentals=0),
    )(*parts, factors, keys, *more)


def lower_kernel(
    place_ref, total_ref, spare0_ref, spare1_ref, spare2_ref, spare3_ref, down_ref,
    zero_ref, rest0_ref, rest1_ref, rest2_ref, rest3_ref, out_ref,
):
    columns = down_columns(place_ref, down_ref)
    spares = (spare0_ref, spare1_ref, spare2_ref, spare3_ref)

    def piece(p, at):
        here = slice(at, at + LANES)
        rows = lambda m, i: spares[m][2 * p + i : 2 * p + i + 1, here]
        value = total_ref[p, :, here]
        if p == 0:
            for rest in (rest0_ref, rest1_ref, rest2_ref, rest3_ref):
                value = value + rest[:, here]
        else:
            value = value + zero_ref[:, here]
        return lowered(value, rows, columns)

    spread_rows(piece, out_ref)


def lower_call(place, total, spares, down, zero, rests):
    out = (SLOTS, Q_DEV, LANES)
    return pl.pallas_call(
        lower_kernel,
        in_specs=[PLACE] + [pl.BlockSpec(memory_space=pltpu.VMEM)] * 11,
        out_specs=pl.BlockSpec(memory_space=pltpu.VMEM),
        out_shape=jax.ShapeDtypeStruct(out, F32),
        compiler_params=pltpu.CompilerParams(vmem_limit_bytes=VMEM_BYTES),
        cost_estimate=pl.CostEstimate(flops=1000000, bytes_accessed=400000, transcendentals=0),
    )(place, total, *spares, down, zero, *rests)


def inverse_columns_kernel(in_ref, table_ref, out_ref, hold_ref):
    result = column_transform(in_ref, table_ref, hold_ref)
    for h in range(2):
        parts = [result[i][:, h * LANES : (h + 1) * LANES] for i in range(16)]
        for g, part in enumerate(exchange(parts, (6, 5, 4, 3))):
            out_ref[h * 16 + g] = part[:Q_DEV]


def inverse_rows_kernel(in_ref, table_ref, out_ref, hold_ref):
    hold_ref[...] = jnp.zeros_like(hold_ref)
    for h in range(2):
        parts = exchange([in_ref[h * 16 + c] for c in range(16)], (6, 2, 1, 0))
        for i, part in enumerate(parts):
            hold_ref[i, 0:Q_DEV, h * LANES : (h + 1) * LANES] = part
    result = transform(hold_ref[...].reshape(128, SIDE), table_ref).reshape(16, 8, SIDE)
    for p in range(2):
        for r in range(8):
            out_ref[0, :, p, r * SIDE : (r + 1) * SIDE] = result[p * 8 + r][:Q_DEV]


def swap(values, axis):
    return lax.all_to_all(values, axis, split_axis=0, concat_axis=0, tiled=True)


def shifted(block, distance):
    route = [(i, (i + distance) % SLOTS) for i in range(SLOTS)]
    return lax.ppermute(block, "slot", route)


def forward(ciphertexts):
    col_fwd, row_fwd, _, _ = dct_constants()
    hold = [pltpu.VMEM((16, 8, SIDE), F32)]
    parts = jnp.transpose(ciphertexts, (0, 2, 1, 3))
    sent = call(rows_kernel, [(SLOTS, Q_DEV, LANES)], parts)
    held = swap(sent, "slot")
    sent = call(
        columns_kernel, [(SLOTS, 2, Q_DEV, LANES)], held, col_fwd, scratch=hold, flops=50000000
    )
    held = swap(sent, "slot")
    return call(
        evals_kernel,
        [(Q_DEV, HALO), (Q_DEV, HALO), (3, 2, HALO)],
        held,
        row_fwd,
        scratch=[pltpu.VMEM((32, 8, SIDE), F32)],
        flops=100000000,
    )


def inverse(sent):
    _, _, col_inv, row_inv = dct_constants()
    hold = [pltpu.VMEM((16, 8, SIDE), F32)]
    held = swap(sent, "slot")
    sent = call(
        inverse_columns_kernel,
        [(SLOTS, Q_DEV, LANES)],
        held,
        col_inv,
        scratch=hold,
        flops=50000000,
    )
    held = swap(sent, "slot")
    out = call(
        inverse_rows_kernel,
        [(1, Q_DEV, 2, POINTS_DEV)],
        held,
        row_inv,
        scratch=hold,
        flops=50000000,
    )
    return jnp.transpose(out, (0, 2, 1, 3))


def gathered(block):
    routes = [[(i, (i + m) % GROUPS) for i in range(GROUPS)] for m in range(GROUPS)]
    return [block] + [lax.ppermute(block, "limb", routes[m]) for m in range(1, GROUPS)]


def after(values, others):
    return lax.optimization_barrier((*values, *others))[: len(values)]


def together(*groups):
    flat = lax.optimization_barrier([value for group in groups for value in group])
    return [[flat.pop(0) for _ in group] for group in groups]


def per_device(ciphertexts, diagonals, baby_keys, giant_keys, up, down):
    place = lax.axis_index("limb").astype(jnp.int32).reshape(1)
    e0, e1, sent = forward(ciphertexts)
    evals = [e1] + gathered(sent)[1:]
    (late_up,), _ = together([up], [e1])
    factors, giant_factors = factors_call(place, late_up)
    kept, spare0, spare1 = products_call(evals, factors, baby_keys)
    *sends, zero, four = babies_call(1, place, kept, gathered(spare1), e1, down, diagonals)
    spares0 = gathered(spare0)
    gots = [shifted(send, r + 1) for r, send in enumerate(sends)]
    sums = babies_call(0, place, kept, spares0, e0, down, diagonals)
    low, high = sums
    gots, (low,) = together(gots, [low])
    shapes = [(9, 2, POINTS_DEV), (24, POINTS_DEV)]
    near, far = call(sort_kernel, shapes, *gots, four, flops=10000)
    far = shifted(far, 4)
    high = shifted(high, 4)
    nears = gathered(near)
    nears[1:], (far,) = together(nears[1:], [far])
    (before,) = giants_call(1, nears, giant_factors, giant_keys)
    (high,), (before,) = together([high], [before])
    rests = call(pair_sum_kernel, [(Q_DEV, POINTS_DEV)] * 4, low, high, flops=10000)
    rests = [rests[0]] + [shifted(rests[r], r) for r in range(1, 4)]
    total, spare = giants_call(4, gathered(far), giant_factors, giant_keys, before)
    return inverse(lower_call(place, total, gathered(spare), down, zero, rests))


def solution(mesh):
    placed = (
        P("ct", None, "limb", "slot"),
        P(None, None, "limb", "slot"),
        P(None, None, None, "limb", "slot"),
        P(None, None, None, "limb", "slot"),
        P("limb", None),
        P("limb", None),
    )
    return jax.shard_map(
        per_device,
        mesh=mesh,
        in_specs=placed,
        out_specs=P("ct", None, "limb", "slot"),
        check_vma=False,
    )
```

```python
import functools

import numpy as np
import jax
import jax.numpy as jnp
import ml_dtypes
from jax import lax
from jax.experimental import pallas as pl
from jax.experimental.pallas import tpu as pltpu
from jax.sharding import PartitionSpec as P

SIDE = 256
DNUM = 3
BABY = 8
GIANT = 8
Q_DEV = 6
LANES = 128
POINTS_DEV = 2048
HALO = 2 * POINTS_DEV
SLOTS = 32
GROUPS = 4
CHUNK = 2048
VMEM_BYTES = 28 * 1024 * 1024
F32 = jnp.float32
BF16 = jnp.bfloat16


def split_constant(values):
    high = values.astype(ml_dtypes.bfloat16)
    low = (values - high.astype(np.float64)).astype(ml_dtypes.bfloat16)
    return np.stack([high, low])


def cosine_matrix():
    k = np.arange(SIDE, dtype=np.float64)[:, None]
    n = np.arange(SIDE, dtype=np.float64)[None, :]
    scale = np.where(k == 0, np.sqrt(1.0 / SIDE), np.sqrt(2.0 / SIDE))
    return scale * np.cos(np.pi * (n + 0.5) * k / SIDE)


def lane_orders():
    lane = np.arange(SIDE)
    half, low = lane // LANES, lane % LANES
    block, rest = low // 64, low % 64
    rows = half * 128 + block * 64 + (rest % 8) * 8 + rest // 8
    cols_fwd = half * 128 + (low % 16) * 8 + low // 16
    c = (low // 64) * 8 + low % 8
    k = (low // 8) % 8
    cols_inv = half * 128 + c * 8 + k
    return rows, cols_fwd, cols_inv


def dct_constants():
    c = cosine_matrix()
    rows, cols_fwd, cols_inv = lane_orders()
    return (
        split_constant(c.T[rows]),
        split_constant(c.T[cols_fwd]),
        split_constant(c[rows]),
        split_constant(c[cols_inv]),
    )


def exchange(values, bits, axis=1):
    values = list(values)
    size = values[0].shape[axis]
    index = lax.broadcasted_iota(jnp.int32, values[0].shape, axis)
    for place, bit in enumerate(reversed(bits)):
        step, span = 1 << place, 1 << bit
        keep = (index & span) == 0
        for i in range(len(values)):
            if i & step:
                continue
            a, b = values[i], values[i + step]
            values[i] = jnp.where(keep, a, pltpu.roll(b, span, axis))
            values[i + step] = jnp.where(keep, pltpu.roll(a, size - span, axis), b)
    return values


def halves(values):
    high = values.astype(BF16)
    return high, (values - high.astype(F32)).astype(BF16)


def matmul(a, b):
    return lax.dot_general(a, b, (((1,), (0,)), ((), ())), preferred_element_type=F32)


def exact_matmul(a, b):
    return lax.dot_general(
        a,
        b,
        (((1,), (0,)), ((), ())),
        precision=lax.Precision.HIGHEST,
        preferred_element_type=F32,
    )


def transform(values, table):
    high, low = halves(values)
    return matmul(high, table[0]) + matmul(low, table[0]) + matmul(high, table[1])


def call(kernel, out_shapes, *args, scratch=(), flops=1000000):
    shapes = [jax.ShapeDtypeStruct(s, F32) for s in out_shapes]
    return pl.pallas_call(
        kernel,
        out_shape=shapes if len(shapes) > 1 else shapes[0],
        scratch_shapes=list(scratch),
        compiler_params=pltpu.CompilerParams(vmem_limit_bytes=VMEM_BYTES),
        cost_estimate=pl.CostEstimate(flops=flops, bytes_accessed=400000, transcendentals=0),
    )(*args)


def group_of(place_ref, m):
    return (place_ref[0] - m) & 3


def down_columns(place_ref, down_ref):
    down = down_ref[...]
    lane = lax.broadcasted_iota(jnp.int32, down.shape, 1)
    columns = []
    for m in range(GROUPS):
        for i in range(2):
            pick = jnp.where(lane == 2 * group_of(place_ref, m) + i, down, 0.0)
            column = jnp.sum(pick, axis=1, keepdims=True)
            columns.append(jnp.broadcast_to(column, (Q_DEV, LANES)))
    return columns


def lowered(kept, rows, columns):
    total = kept
    for g in range(GROUPS):
        for i in range(2):
            total = total - columns[2 * g + i] * rows(g, i)
    return total


def spread_rows(piece, out_ref):
    for h in range(2):
        parts = [piece(p, r * SIDE + h * LANES) for p in range(2) for r in range(8)]
        for c, part in enumerate(exchange(parts, (6, 5, 4, 3))):
            out_ref[h * 16 + c] = part


def rows_kernel(x_ref, out_ref):
    spread_rows(lambda p, at: x_ref[0, :, p, at : at + LANES], out_ref)


def column_transform(in_ref, table_ref, hold_ref):
    hold_ref[...] = jnp.zeros_like(hold_ref)
    for h in range(2):
        parts = exchange([in_ref[h * 16 + s] for s in range(16)], (6, 2, 1, 0))
        for i, part in enumerate(parts):
            hold_ref[i, 0:Q_DEV, h * LANES : (h + 1) * LANES] = part
    result = transform(hold_ref[...].reshape(128, SIDE), table_ref)
    return result.reshape(16, 8, SIDE)


def columns_kernel(in_ref, table_ref, out_ref, hold_ref):
    result = column_transform(in_ref, table_ref, hold_ref)
    lane = lax.broadcasted_iota(jnp.int32, (8, LANES), 1)
    first = (lane & 8) == 0
    for p in range(2):
        pairs = []
        for h in range(2):
            parts = [result[p * 8 + k][:, h * LANES : (h + 1) * LANES] for k in range(8)]
            pairs += exchange(parts, (6, 5, 4))
        for i in range(16):
            out_ref[2 * i + 1, p] = pairs[i][:Q_DEV]
            both = jnp.where(
                first, pltpu.roll(pairs[i - 1], LANES - 8, 1), pltpu.roll(pairs[i], 8, 1)
            )
            out_ref[2 * i, p] = both[:Q_DEV]


def evals_kernel(in_ref, table_ref, e0_ref, e1_ref, sent_ref, hold_ref):
    hold_ref[...] = jnp.zeros_like(hold_ref)
    for p in range(2):
        for h in range(2):
            parts = exchange([in_ref[h * 16 + c, p] for c in range(16)], (3, 2, 1, 0))
            for row, part in enumerate(parts):
                hold_ref[p * 16 + row, 0:Q_DEV, h * LANES : (h + 1) * LANES] = part
    result = transform(hold_ref[...].reshape(256, SIDE), table_ref).reshape(32, 8, SIDE)
    for row in range(16):
        at = slice(row * SIDE, (row + 1) * SIDE)
        e0_ref[:, at] = result[row][:Q_DEV]
        e1_ref[:, at] = result[16 + row][:Q_DEV]
        for i in range(3):
            sent_ref[i, :, at] = result[16 + row][2 * i : 2 * i + 2]


def factors_kernel(place_ref, up_ref, baby_ref, giant_ref):
    iota = lambda shape, axis: lax.broadcasted_iota(jnp.int32, shape, axis)
    up = up_ref[...]

    def spread(held, limb, columns):
        pick = (iota((24, columns), 0) == limb).astype(F32)
        wide = exact_matmul(up, pick)
        digit = limb[0:8] >> 3
        return [jnp.where(held[0:8] & (digit == d), wide, 0.0) for d in range(DNUM)]

    q = iota((24, 32), 1)
    used = (q & 7) < Q_DEV
    limb = jnp.where(used, 6 * group_of(place_ref, q >> 3) + (q & 7), -8)
    fh, fl = halves(jnp.concatenate(spread(used, limb, 32), axis=0))
    baby_ref[...] = jnp.concatenate([fh, fh, fl], axis=1).astype(F32)
    q = iota((24, 96), 1)
    block = (q >= 24).astype(jnp.int32) + (q >= 48) + (q >= 72)
    rest = q - 24 * block
    giant = (rest * 43) >> 8
    limb = 6 * group_of(place_ref, block) + rest - 6 * giant
    for j in range(4):
        at = slice(j * 24, j * 24 + 24)
        fh, fl = halves(jnp.concatenate(spread(giant == j, limb, 96), axis=0))
        giant_ref[0, at], giant_ref[1, at] = fh.astype(F32), fl.astype(F32)


def factors_call(place, up):
    return pl.pallas_call(
        factors_kernel,
        in_specs=[pl.BlockSpec(memory_space=pltpu.SMEM), pl.BlockSpec(memory_space=pltpu.VMEM)],
        out_specs=[pl.BlockSpec(memory_space=pltpu.VMEM)] * 2,
        out_shape=[
            jax.ShapeDtypeStruct((24, 96), F32),
            jax.ShapeDtypeStruct((2, 96, 96), F32),
        ],
        compiler_params=pltpu.CompilerParams(vmem_limit_bytes=VMEM_BYTES),
        cost_estimate=pl.CostEstimate(flops=1000000, bytes_accessed=100000, transcendentals=0),
    )(place, up)


def products_kernel(
    e1a_ref, e1b_ref, e1c_ref, e1d_ref, factors_ref, keys_ref,
    kept_ref, spare0_ref, spare1_ref, raised_ref, stage_ref,
):
    step = pl.program_id(0)

    @pl.when(step == 0)
    def _():
        lhs = factors_ref[...].astype(BF16)
        stage_ref[...] = jnp.zeros_like(stage_ref)
        stage_ref[0:Q_DEV, :] = e1a_ref[...]
        for m, ref in enumerate((e1b_ref, e1c_ref, e1d_ref), 1):
            for i in range(3):
                stage_ref[8 * m + 2 * i : 8 * m + 2 * i + 2, :] = ref[i]
        for part in range(8):
            at = slice(part * 512, (part + 1) * 512)
            eh, el = halves(stage_ref[:, at])
            raised_ref[:, at] = matmul(lhs, jnp.concatenate([eh, el, eh], axis=0))

    spares = (spare0_ref, spare1_ref)

    def body(t, carry):
        base = pl.multiple_of(step * CHUNK + t * LANES, LANES)
        here = pl.ds(pl.multiple_of(t * LANES, LANES), LANES)
        for k in range(1, BABY):
            at = pl.ds(base + (8 - k) * SIDE, LANES)
            views = [raised_ref[d * 8 : d * 8 + 8, at] for d in range(DNUM)]
            for s in range(2):
                total = None
                for d in range(DNUM):
                    term = views[d] * keys_ref[k - 1, d, s, :, here].astype(F32)
                    total = term if total is None else total + term
                kept_ref[s, k - 1, :, here] = total
                spares[s][k - 1, :, here] = total[Q_DEV:]
        return carry

    lax.fori_loop(0, CHUNK // LANES, body, 0)


def babies_kernel(
    poly, place_ref, kept_ref, spare0_ref, spare1_ref, spare2_ref, spare3_ref,
    evals_ref, down_ref, diag_ref, *out_refs,
):
    step = pl.program_id(0)
    columns = down_columns(place_ref, down_ref)
    spares = (spare0_ref, spare1_ref, spare2_ref, spare3_ref)

    def body(t, carry):
        base = pl.multiple_of(step * CHUNK + t * LANES, LANES)
        here = pl.ds(pl.multiple_of(t * LANES, LANES), LANES)
        babies = [evals_ref[:, pl.ds(base + POINTS_DEV, LANES)]]
        for k in range(1, BABY):
            rows = lambda m, i: spares[m][k - 1, i : i + 1, here]
            baby = lowered(kept_ref[0, k - 1, 0:Q_DEV, here], rows, columns)
            if poly == 0:
                baby = baby + evals_ref[:, pl.ds(base + (8 - k) * SIDE, LANES)]
            babies.append(baby)
        for j in range(GIANT):
            inner = None
            for k in range(BABY):
                term = diag_ref[j, k, :, here].astype(F32) * babies[k]
                inner = term if inner is None else inner + term
            if poly == 0:
                at = 6 * (j % 4)
                out_refs[j // 4][at : at + 6, here] = inner
            elif j % 4 == 0:
                out_refs[3 + j // 4][:, here] = inner
            else:
                for i in range(3):
                    out_refs[j % 4 - 1][3 * (j // 4) + i, :, here] = inner[2 * i : 2 * i + 2]
        return carry

    lax.fori_loop(0, CHUNK // LANES, body, 0)


def whole(a):
    return pl.BlockSpec(a.shape, lambda i, n=a.ndim: (0,) * n)


def lanes(*lead):
    return pl.BlockSpec(lead + (CHUNK,), lambda i, n=len(lead): (0,) * n + (i,))


PLACE = pl.BlockSpec(memory_space=pltpu.SMEM)


def products_call(evals, factors, keys):
    return pl.pallas_call(
        products_kernel,
        grid=(POINTS_DEV // CHUNK,),
        in_specs=[whole(e) for e in evals] + [whole(factors), lanes(7, 3, 2, 8)],
        out_specs=[lanes(2, 7, 8), lanes(7, 2), lanes(7, 2)],
        out_shape=[
            jax.ShapeDtypeStruct((2, 7, 8, POINTS_DEV), F32),
            jax.ShapeDtypeStruct((7, 2, POINTS_DEV), F32),
            jax.ShapeDtypeStruct((7, 2, POINTS_DEV), F32),
        ],
        scratch_shapes=[pltpu.VMEM((24, HALO), F32), pltpu.VMEM((32, HALO), F32)],
        compiler_params=pltpu.CompilerParams(vmem_limit_bytes=VMEM_BYTES),
        cost_estimate=pl.CostEstimate(flops=40000000, bytes_accessed=4000000, transcendentals=0),
    )(*evals, factors, keys)


def babies_call(poly, place, kept, spares, evals, down, diagonals):
    rows = [(24,), (24,)] if poly == 0 else [(6, 2)] * 3 + [(6,)] * 2
    part = pl.BlockSpec((1, 7, 8, CHUNK), lambda i: (poly, 0, 0, i))
    return pl.pallas_call(
        functools.partial(babies_kernel, poly),
        grid=(POINTS_DEV // CHUNK,),
        in_specs=[PLACE, part]
        + [lanes(7, 2)] * 4
        + [whole(evals), whole(down), lanes(8, 8, Q_DEV)],
        out_specs=[lanes(*r) for r in rows],
        out_shape=[jax.ShapeDtypeStruct((*r, POINTS_DEV), F32) for r in rows],
        compiler_params=pltpu.CompilerParams(vmem_limit_bytes=VMEM_BYTES),
        cost_estimate=pl.CostEstimate(flops=40000000, bytes_accessed=6000000, transcendentals=0),
    )(place, kept, *spares, evals, down, diagonals)


def sort_kernel(got1_ref, got2_ref, got3_ref, four_ref, near_ref, far_ref):
    far_ref[0:6, :] = four_ref[...]
    for r, got in enumerate((got1_ref, got2_ref, got3_ref)):
        for i in range(3):
            near_ref[3 * r + i] = got[i]
            far_ref[6 + 6 * r + 2 * i : 8 + 6 * r + 2 * i, :] = got[3 + i]


def pair_sum_kernel(low_ref, high_ref, *out_refs):
    for r, out_ref in enumerate(out_refs):
        at = slice(6 * r, 6 * r + 6)
        out_ref[...] = low_ref[at, :] + high_ref[at, :]


def giants_kernel(
    first, part0_ref, part1_ref, part2_ref, part3_ref, factor_ref, keys_ref, *refs
):
    before_ref = spare_ref = None
    if first == 1:
        total_ref, raised_ref, stage_ref = refs
    else:
        before_ref, total_ref, spare_ref, raised_ref = refs
    fh, fl = factor_ref[0].astype(BF16), factor_ref[1].astype(BF16)
    parts = (part0_ref, part1_ref, part2_ref, part3_ref)
    if first == 1:
        for m, ref in enumerate(parts):
            for i in range(9):
                stage_ref[24 * m + 2 * i : 24 * m + 2 * i + 2, :] = ref[i]
            stage_ref[24 * m + 18 : 24 * m + 24, :] = jnp.zeros((6, CHUNK), F32)
        held = stage_ref[...]
    else:
        held = jnp.concatenate([ref[...] for ref in parts], axis=0)
    eh, el = halves(held)
    raised_ref[...] = matmul(fh, eh) + matmul(fh, el) + matmul(fl, eh)

    def body(t, carry):
        here = pl.ds(pl.multiple_of(t * LANES, LANES), LANES)
        sums = [None, None]
        if before_ref is not None:
            sums = [before_ref[s, :, here] for s in range(2)]
        for j in range(3 if first == 1 else 4):
            for d in range(DNUM):
                at = j * 24 + d * 8
                value = raised_ref[at : at + 8, here]
                for s in range(2):
                    key = keys_ref[first - 1 + j, d, s, :, here].astype(F32)
                    sums[s] = value * key if sums[s] is None else sums[s] + value * key
        if before_ref is None:
            total_ref[0, :, here], total_ref[1, :, here] = sums
        else:
            for s in range(2):
                total_ref[s, :, here] = sums[s][:Q_DEV]
                spare_ref[2 * s : 2 * s + 2, here] = sums[s][Q_DEV:]
        return carry

    lax.fori_loop(0, CHUNK // LANES, body, 0)


def giants_call(first, parts, factors, keys, before=None):
    more = [] if before is None else [before]
    shapes = [(2, 8)] if before is None else [(2, Q_DEV), (4,)]
    return pl.pallas_call(
        functools.partial(giants_kernel, first),
        grid=(POINTS_DEV // CHUNK,),
        in_specs=[lanes(9, 2) if first == 1 else lanes(24)] * 4
        + [whole(factors), lanes(7, 3, 2, 8)]
        + [lanes(2, 8) for _ in more],
        out_specs=[lanes(*shape) for shape in shapes],
        out_shape=[jax.ShapeDtypeStruct(shape + (POINTS_DEV,), F32) for shape in shapes],
        scratch_shapes=[pltpu.VMEM((96, CHUNK), F32)] * (2 if first == 1 else 1),
        compiler_params=pltpu.CompilerParams(vmem_limit_bytes=VMEM_BYTES),
        cost_estimate=pl.CostEstimate(flops=20000000, bytes_accessed=2000000, transcendentals=0),
    )(*parts, factors, keys, *more)


def lower_kernel(
    place_ref, total_ref, spare0_ref, spare1_ref, spare2_ref, spare3_ref, down_ref,
    zero_ref, rest0_ref, rest1_ref, rest2_ref, rest3_ref, out_ref,
):
    columns = down_columns(place_ref, down_ref)
    spares = (spare0_ref, spare1_ref, spare2_ref, spare3_ref)

    def piece(p, at):
        here = slice(at, at + LANES)
        rows = lambda m, i: spares[m][2 * p + i : 2 * p + i + 1, here]
        value = total_ref[p, :, here]
        if p == 0:
            for rest in (rest0_ref, rest1_ref, rest2_ref, rest3_ref):
                value = value + rest[:, here]
        else:
            value = value + zero_ref[:, here]
        return lowered(value, rows, columns)

    spread_rows(piece, out_ref)


def lower_call(place, total, spares, down, zero, rests):
    out = (SLOTS, Q_DEV, LANES)
    return pl.pallas_call(
        lower_kernel,
        in_specs=[PLACE] + [pl.BlockSpec(memory_space=pltpu.VMEM)] * 11,
        out_specs=pl.BlockSpec(memory_space=pltpu.VMEM),
        out_shape=jax.ShapeDtypeStruct(out, F32),
        compiler_params=pltpu.CompilerParams(vmem_limit_bytes=VMEM_BYTES),
        cost_estimate=pl.CostEstimate(flops=1000000, bytes_accessed=400000, transcendentals=0),
    )(place, total, *spares, down, zero, *rests)


def inverse_columns_kernel(in_ref, table_ref, out_ref, hold_ref):
    result = column_transform(in_ref, table_ref, hold_ref)
    for h in range(2):
        parts = [result[i][:, h * LANES : (h + 1) * LANES] for i in range(16)]
        for g, part in enumerate(exchange(parts, (6, 5, 4, 3))):
            out_ref[h * 16 + g] = part[:Q_DEV]


def inverse_rows_kernel(in_ref, table_ref, out_ref, hold_ref):
    hold_ref[...] = jnp.zeros_like(hold_ref)
    for h in range(2):
        parts = exchange([in_ref[h * 16 + c] for c in range(16)], (6, 2, 1, 0))
        for i, part in enumerate(parts):
            hold_ref[i, 0:Q_DEV, h * LANES : (h + 1) * LANES] = part
    result = transform(hold_ref[...].reshape(128, SIDE), table_ref).reshape(16, 8, SIDE)
    for p in range(2):
        for r in range(8):
            out_ref[0, :, p, r * SIDE : (r + 1) * SIDE] = result[p * 8 + r][:Q_DEV]


def swap(values, axis):
    return lax.all_to_all(values, axis, split_axis=0, concat_axis=0, tiled=True)


def shifted(block, distance):
    route = [(i, (i + distance) % SLOTS) for i in range(SLOTS)]
    return lax.ppermute(block, "slot", route)


def forward(ciphertexts):
    col_fwd, row_fwd, _, _ = dct_constants()
    hold = [pltpu.VMEM((16, 8, SIDE), F32)]
    parts = jnp.transpose(ciphertexts, (0, 2, 1, 3))
    sent = call(rows_kernel, [(SLOTS, Q_DEV, LANES)], parts)
    held = swap(sent, "slot")
    sent = call(
        columns_kernel, [(SLOTS, 2, Q_DEV, LANES)], held, col_fwd, scratch=hold, flops=50000000
    )
    held = swap(sent, "slot")
    return call(
        evals_kernel,
        [(Q_DEV, HALO), (Q_DEV, HALO), (3, 2, HALO)],
        held,
        row_fwd,
        scratch=[pltpu.VMEM((32, 8, SIDE), F32)],
        flops=100000000,
    )


def inverse(sent):
    _, _, col_inv, row_inv = dct_constants()
    hold = [pltpu.VMEM((16, 8, SIDE), F32)]
    held = swap(sent, "slot")
    sent = call(
        inverse_columns_kernel,
        [(SLOTS, Q_DEV, LANES)],
        held,
        col_inv,
        scratch=hold,
        flops=50000000,
    )
    held = swap(sent, "slot")
    out = call(
        inverse_rows_kernel,
        [(1, Q_DEV, 2, POINTS_DEV)],
        held,
        row_inv,
        scratch=hold,
        flops=50000000,
    )
    return jnp.transpose(out, (0, 2, 1, 3))


def gathered(block):
    routes = [[(i, (i + m) % GROUPS) for i in range(GROUPS)] for m in range(GROUPS)]
    return [block] + [lax.ppermute(block, "limb", routes[m]) for m in range(1, GROUPS)]


def after(values, others):
    return lax.optimization_barrier((*values, *others))[: len(values)]


def together(*groups):
    flat = lax.optimization_barrier([value for group in groups for value in group])
    return [[flat.pop(0) for _ in group] for group in groups]


def per_device(ciphertexts, diagonals, baby_keys, giant_keys, up, down):
    place = lax.axis_index("limb").astype(jnp.int32).reshape(1)
    e0, e1, sent = forward(ciphertexts)
    evals = [e1] + gathered(sent)[1:]
    (late_up,), _ = together([up], [e1])
    factors, giant_factors = factors_call(place, late_up)
    kept, spare0, spare1 = products_call(evals, factors, baby_keys)
    *sends, zero, four = babies_call(1, place, kept, gathered(spare1), e1, down, diagonals)
    spares0 = gathered(spare0)
    gots = [shifted(send, r + 1) for r, send in enumerate(sends)]
    sums = babies_call(0, place, kept, spares0, e0, down, diagonals)
    low, high = sums
    gots, (low,) = together(gots, [low])
    shapes = [(9, 2, POINTS_DEV), (24, POINTS_DEV)]
    near, far = call(sort_kernel, shapes, *gots, four, flops=10000)
    far = shifted(far, 4)
    high = shifted(high, 4)
    nears = gathered(near)
    nears[1:], (far,) = together(nears[1:], [far])
    (before,) = giants_call(1, nears, giant_factors, giant_keys)
    (high,), (before,) = together([high], [before])
    rests = call(pair_sum_kernel, [(Q_DEV, POINTS_DEV)] * 4, low, high, flops=10000)
    rests = [rests[0]] + [shifted(rests[r], r) for r in range(1, 4)]
    total, spare = giants_call(4, gathered(far), giant_factors, giant_keys, before)
    return inverse(lower_call(place, total, gathered(spare), down, zero, rests))


def solution(mesh):
    placed = (
        P("ct", None, "limb", "slot"),
        P(None, None, "limb", "slot"),
        P(None, None, None, "limb", "slot"),
        P(None, None, None, "limb", "slot"),
        P("limb", None),
        P("limb", None),
    )
    return jax.shard_map(
        per_device,
        mesh=mesh,
        in_specs=placed,
        out_specs=P("ct", None, "limb", "slot"),
        check_vma=False,
    )
```

```python
import functools

import numpy as np
import jax
import jax.numpy as jnp
import ml_dtypes
from jax import lax
from jax.experimental import pallas as pl
from jax.experimental.pallas import tpu as pltpu
from jax.sharding import PartitionSpec as P

SIDE = 256
DNUM = 3
BABY = 8
GIANT = 8
Q_DEV = 6
LANES = 128
POINTS_DEV = 2048
HALO = 2 * POINTS_DEV
SLOTS = 32
GROUPS = 4
CHUNK = 2048
VMEM_BYTES = 28 * 1024 * 1024
F32 = jnp.float32
BF16 = jnp.bfloat16


def split_constant(values):
    high = values.astype(ml_dtypes.bfloat16)
    low = (values - high.astype(np.float64)).astype(ml_dtypes.bfloat16)
    return np.stack([high, low])


def cosine_matrix():
    k = np.arange(SIDE, dtype=np.float64)[:, None]
    n = np.arange(SIDE, dtype=np.float64)[None, :]
    scale = np.where(k == 0, np.sqrt(1.0 / SIDE), np.sqrt(2.0 / SIDE))
    return scale * np.cos(np.pi * (n + 0.5) * k / SIDE)


def lane_orders():
    lane = np.arange(SIDE)
    half, low = lane // LANES, lane % LANES
    block, rest = low // 64, low % 64
    rows = half * 128 + block * 64 + (rest % 8) * 8 + rest // 8
    cols_fwd = half * 128 + (low % 16) * 8 + low // 16
    c = (low // 64) * 8 + low % 8
    k = (low // 8) % 8
    cols_inv = half * 128 + c * 8 + k
    return rows, cols_fwd, cols_inv


def dct_constants():
    c = cosine_matrix()
    rows, cols_fwd, cols_inv = lane_orders()
    return (
        split_constant(c.T[rows]),
        split_constant(c.T[cols_fwd]),
        split_constant(c[rows]),
        split_constant(c[cols_inv]),
    )


def exchange(values, bits, axis=1):
    values = list(values)
    size = values[0].shape[axis]
    index = lax.broadcasted_iota(jnp.int32, values[0].shape, axis)
    for place, bit in enumerate(reversed(bits)):
        step, span = 1 << place, 1 << bit
        keep = (index & span) == 0
        for i in range(len(values)):
            if i & step:
                continue
            a, b = values[i], values[i + step]
            values[i] = jnp.where(keep, a, pltpu.roll(b, span, axis))
            values[i + step] = jnp.where(keep, pltpu.roll(a, size - span, axis), b)
    return values


def halves(values):
    high = values.astype(BF16)
    return high, (values - high.astype(F32)).astype(BF16)


def matmul(a, b):
    return lax.dot_general(a, b, (((1,), (0,)), ((), ())), preferred_element_type=F32)


def exact_matmul(a, b):
    return lax.dot_general(
        a,
        b,
        (((1,), (0,)), ((), ())),
        precision=lax.Precision.HIGHEST,
        preferred_element_type=F32,
    )


def transform(values, table):
    high, low = halves(values)
    return matmul(high, table[0]) + matmul(low, table[0]) + matmul(high, table[1])


def call(kernel, out_shapes, *args, scratch=(), flops=1000000):
    shapes = [jax.ShapeDtypeStruct(s, F32) for s in out_shapes]
    return pl.pallas_call(
        kernel,
        out_shape=shapes if len(shapes) > 1 else shapes[0],
        scratch_shapes=list(scratch),
        compiler_params=pltpu.CompilerParams(vmem_limit_bytes=VMEM_BYTES),
        cost_estimate=pl.CostEstimate(flops=flops, bytes_accessed=400000, transcendentals=0),
    )(*args)


def group_of(place_ref, m):
    return (place_ref[0] - m) & 3


def down_columns(place_ref, down_ref):
    down = down_ref[...]
    lane = lax.broadcasted_iota(jnp.int32, down.shape, 1)
    columns = []
    for m in range(GROUPS):
        for i in range(2):
            pick = jnp.where(lane == 2 * group_of(place_ref, m) + i, down, 0.0)
            column = jnp.sum(pick, axis=1, keepdims=True)
            columns.append(jnp.broadcast_to(column, (Q_DEV, LANES)))
    return columns


def lowered(kept, rows, columns):
    total = kept
    for g in range(GROUPS):
        for i in range(2):
            total = total - columns[2 * g + i] * rows(g, i)
    return total


def spread_rows(piece, out_ref):
    for h in range(2):
        parts = [piece(p, r * SIDE + h * LANES) for p in range(2) for r in range(8)]
        for c, part in enumerate(exchange(parts, (6, 5, 4, 3))):
            out_ref[h * 16 + c] = part


def rows_kernel(x_ref, out_ref):
    spread_rows(lambda p, at: x_ref[0, :, p, at : at + LANES], out_ref)


def column_transform(in_ref, table_ref, hold_ref):
    hold_ref[...] = jnp.zeros_like(hold_ref)
    for h in range(2):
        parts = exchange([in_ref[h * 16 + s] for s in range(16)], (6, 2, 1, 0))
        for i, part in enumerate(parts):
            hold_ref[i, 0:Q_DEV, h * LANES : (h + 1) * LANES] = part
    result = transform(hold_ref[...].reshape(128, SIDE), table_ref)
    return result.reshape(16, 8, SIDE)


def columns_kernel(in_ref, table_ref, out_ref, hold_ref):
    result = column_transform(in_ref, table_ref, hold_ref)
    lane = lax.broadcasted_iota(jnp.int32, (8, LANES), 1)
    first = (lane & 8) == 0
    for p in range(2):
        pairs = []
        for h in range(2):
            parts = [result[p * 8 + k][:, h * LANES : (h + 1) * LANES] for k in range(8)]
            pairs += exchange(parts, (6, 5, 4))
        for i in range(16):
            out_ref[2 * i + 1, p] = pairs[i][:Q_DEV]
            both = jnp.where(
                first, pltpu.roll(pairs[i - 1], LANES - 8, 1), pltpu.roll(pairs[i], 8, 1)
            )
            out_ref[2 * i, p] = both[:Q_DEV]


def evals_kernel(poly, in_ref, table_ref, *refs):
    *out_refs, hold_ref = refs
    hold_ref[...] = jnp.zeros_like(hold_ref)
    for h in range(2):
        parts = exchange([in_ref[h * 16 + c, poly] for c in range(16)], (3, 2, 1, 0))
        for row, part in enumerate(parts):
            hold_ref[row, 0:Q_DEV, h * LANES : (h + 1) * LANES] = part
    result = transform(hold_ref[...].reshape(128, SIDE), table_ref).reshape(16, 8, SIDE)
    for row in range(16):
        at = slice(row * SIDE, (row + 1) * SIDE)
        out_refs[0][:, at] = result[row][:Q_DEV]
        if poly == 1:
            for i in range(3):
                out_refs[1][i, :, at] = result[row][2 * i : 2 * i + 2]


def factors_kernel(place_ref, up_ref, baby_ref, giant_ref):
    iota = lambda shape, axis: lax.broadcasted_iota(jnp.int32, shape, axis)
    up = up_ref[...]

    def spread(held, limb, columns):
        pick = (iota((24, columns), 0) == limb).astype(F32)
        wide = exact_matmul(up, pick)
        digit = limb[0:8] >> 3
        return [jnp.where(held[0:8] & (digit == d), wide, 0.0) for d in range(DNUM)]

    q = iota((24, 32), 1)
    used = (q & 7) < Q_DEV
    limb = jnp.where(used, 6 * group_of(place_ref, q >> 3) + (q & 7), -8)
    fh, fl = halves(jnp.concatenate(spread(used, limb, 32), axis=0))
    baby_ref[...] = jnp.concatenate([fh, fh, fl], axis=1).astype(F32)
    q = iota((24, 96), 1)
    block = (q >= 24).astype(jnp.int32) + (q >= 48) + (q >= 72)
    rest = q - 24 * block
    giant = (rest * 43) >> 8
    limb = 6 * group_of(place_ref, block) + rest - 6 * giant
    for j in range(4):
        at = slice(j * 24, j * 24 + 24)
        fh, fl = halves(jnp.concatenate(spread(giant == j, limb, 96), axis=0))
        giant_ref[0, at], giant_ref[1, at] = fh.astype(F32), fl.astype(F32)


def factors_call(place, up):
    return pl.pallas_call(
        factors_kernel,
        in_specs=[pl.BlockSpec(memory_space=pltpu.SMEM), pl.BlockSpec(memory_space=pltpu.VMEM)],
        out_specs=[pl.BlockSpec(memory_space=pltpu.VMEM)] * 2,
        out_shape=[
            jax.ShapeDtypeStruct((24, 96), F32),
            jax.ShapeDtypeStruct((2, 96, 96), F32),
        ],
        compiler_params=pltpu.CompilerParams(vmem_limit_bytes=VMEM_BYTES),
        cost_estimate=pl.CostEstimate(flops=1000000, bytes_accessed=100000, transcendentals=0),
    )(place, up)


def products_kernel(
    e1a_ref, e1b_ref, e1c_ref, e1d_ref, factors_ref, keys_ref,
    kept_ref, spare0_ref, spare1_ref, raised_ref, stage_ref,
):
    step = pl.program_id(0)

    @pl.when(step == 0)
    def _():
        lhs = factors_ref[...].astype(BF16)
        stage_ref[...] = jnp.zeros_like(stage_ref)
        stage_ref[0:Q_DEV, :] = e1a_ref[...]
        for m, ref in enumerate((e1b_ref, e1c_ref, e1d_ref), 1):
            for i in range(3):
                stage_ref[8 * m + 2 * i : 8 * m + 2 * i + 2, :] = ref[i]
        for part in range(8):
            at = slice(part * 512, (part + 1) * 512)
            eh, el = halves(stage_ref[:, at])
            raised_ref[:, at] = matmul(lhs, jnp.concatenate([eh, el, eh], axis=0))

    spares = (spare0_ref, spare1_ref)

    def body(t, carry):
        base = pl.multiple_of(step * CHUNK + t * LANES, LANES)
        here = pl.ds(pl.multiple_of(t * LANES, LANES), LANES)
        for k in range(1, BABY):
            at = pl.ds(base + (8 - k) * SIDE, LANES)
            views = [raised_ref[d * 8 : d * 8 + 8, at] for d in range(DNUM)]
            for s in range(2):
                total = None
                for d in range(DNUM):
                    term = views[d] * keys_ref[k - 1, d, s, :, here].astype(F32)
                    total = term if total is None else total + term
                kept_ref[s, k - 1, :, here] = total
                spares[s][k - 1, :, here] = total[Q_DEV:]
        return carry

    lax.fori_loop(0, CHUNK // LANES, body, 0)


def babies_kernel(
    poly, place_ref, kept_ref, spare0_ref, spare1_ref, spare2_ref, spare3_ref,
    evals_ref, down_ref, diag_ref, *out_refs,
):
    step = pl.program_id(0)
    columns = down_columns(place_ref, down_ref)
    spares = (spare0_ref, spare1_ref, spare2_ref, spare3_ref)

    def body(t, carry):
        base = pl.multiple_of(step * CHUNK + t * LANES, LANES)
        here = pl.ds(pl.multiple_of(t * LANES, LANES), LANES)
        babies = [evals_ref[:, pl.ds(base + POINTS_DEV, LANES)]]
        for k in range(1, BABY):
            rows = lambda m, i: spares[m][k - 1, i : i + 1, here]
            baby = lowered(kept_ref[0, k - 1, 0:Q_DEV, here], rows, columns)
            if poly == 0:
                baby = baby + evals_ref[:, pl.ds(base + (8 - k) * SIDE, LANES)]
            babies.append(baby)
        for j in range(GIANT):
            inner = None
            for k in range(BABY):
                term = diag_ref[j, k, :, here].astype(F32) * babies[k]
                inner = term if inner is None else inner + term
            if poly == 0:
                at = 6 * (j % 4)
                out_refs[j // 4][at : at + 6, here] = inner
            elif j % 4 == 0:
                out_refs[3 + j // 4][:, here] = inner
            else:
                for i in range(3):
                    out_refs[j % 4 - 1][3 * (j // 4) + i, :, here] = inner[2 * i : 2 * i + 2]
        return carry

    lax.fori_loop(0, CHUNK // LANES, body, 0)


def whole(a):
    return pl.BlockSpec(a.shape, lambda i, n=a.ndim: (0,) * n)


def lanes(*lead):
    return pl.BlockSpec(lead + (CHUNK,), lambda i, n=len(lead): (0,) * n + (i,))


PLACE = pl.BlockSpec(memory_space=pltpu.SMEM)


def products_call(evals, factors, keys):
    return pl.pallas_call(
        products_kernel,
        grid=(POINTS_DEV // CHUNK,),
        in_specs=[whole(e) for e in evals] + [whole(factors), lanes(7, 3, 2, 8)],
        out_specs=[lanes(2, 7, 8), lanes(7, 2), lanes(7, 2)],
        out_shape=[
            jax.ShapeDtypeStruct((2, 7, 8, POINTS_DEV), F32),
            jax.ShapeDtypeStruct((7, 2, POINTS_DEV), F32),
            jax.ShapeDtypeStruct((7, 2, POINTS_DEV), F32),
        ],
        scratch_shapes=[pltpu.VMEM((24, HALO), F32), pltpu.VMEM((32, HALO), F32)],
        compiler_params=pltpu.CompilerParams(vmem_limit_bytes=VMEM_BYTES),
        cost_estimate=pl.CostEstimate(flops=40000000, bytes_accessed=4000000, transcendentals=0),
    )(*evals, factors, keys)


def babies_call(poly, place, kept, spares, evals, down, diagonals):
    rows = [(24,), (24,)] if poly == 0 else [(6, 2)] * 3 + [(6,)] * 2
    part = pl.BlockSpec((1, 7, 8, CHUNK), lambda i: (poly, 0, 0, i))
    return pl.pallas_call(
        functools.partial(babies_kernel, poly),
        grid=(POINTS_DEV // CHUNK,),
        in_specs=[PLACE, part]
        + [lanes(7, 2)] * 4
        + [whole(evals), whole(down), lanes(8, 8, Q_DEV)],
        out_specs=[lanes(*r) for r in rows],
        out_shape=[jax.ShapeDtypeStruct((*r, POINTS_DEV), F32) for r in rows],
        compiler_params=pltpu.CompilerParams(vmem_limit_bytes=VMEM_BYTES),
        cost_estimate=pl.CostEstimate(flops=40000000, bytes_accessed=6000000, transcendentals=0),
    )(place, kept, *spares, evals, down, diagonals)


def sort_kernel(got1_ref, got2_ref, got3_ref, four_ref, near_ref, far_ref):
    far_ref[0:6, :] = four_ref[...]
    for r, got in enumerate((got1_ref, got2_ref, got3_ref)):
        for i in range(3):
            near_ref[3 * r + i] = got[i]
            far_ref[6 + 6 * r + 2 * i : 8 + 6 * r + 2 * i, :] = got[3 + i]


def pair_sum_kernel(low_ref, high_ref, *out_refs):
    for r, out_ref in enumerate(out_refs):
        at = slice(6 * r, 6 * r + 6)
        out_ref[...] = low_ref[at, :] + high_ref[at, :]


def giants_kernel(
    first, part0_ref, part1_ref, part2_ref, part3_ref, factor_ref, keys_ref, *refs
):
    before_ref = spare_ref = None
    if first == 1:
        total_ref, raised_ref, stage_ref = refs
    else:
        before_ref, total_ref, spare_ref, raised_ref = refs
    fh, fl = factor_ref[0].astype(BF16), factor_ref[1].astype(BF16)
    parts = (part0_ref, part1_ref, part2_ref, part3_ref)
    if first == 1:
        for m, ref in enumerate(parts):
            for i in range(9):
                stage_ref[24 * m + 2 * i : 24 * m + 2 * i + 2, :] = ref[i]
            stage_ref[24 * m + 18 : 24 * m + 24, :] = jnp.zeros((6, CHUNK), F32)
        held = stage_ref[...]
    else:
        held = jnp.concatenate([ref[...] for ref in parts], axis=0)
    eh, el = halves(held)
    raised_ref[...] = matmul(fh, eh) + matmul(fh, el) + matmul(fl, eh)

    def body(t, carry):
        here = pl.ds(pl.multiple_of(t * LANES, LANES), LANES)
        sums = [None, None]
        if before_ref is not None:
            sums = [before_ref[s, :, here] for s in range(2)]
        for j in range(3 if first == 1 else 4):
            for d in range(DNUM):
                at = j * 24 + d * 8
                value = raised_ref[at : at + 8, here]
                for s in range(2):
                    key = keys_ref[first - 1 + j, d, s, :, here].astype(F32)
                    sums[s] = value * key if sums[s] is None else sums[s] + value * key
        if before_ref is None:
            total_ref[0, :, here], total_ref[1, :, here] = sums
        else:
            for s in range(2):
                total_ref[s, :, here] = sums[s][:Q_DEV]
                spare_ref[2 * s : 2 * s + 2, here] = sums[s][Q_DEV:]
        return carry

    lax.fori_loop(0, CHUNK // LANES, body, 0)


def giants_call(first, parts, factors, keys, before=None):
    more = [] if before is None else [before]
    shapes = [(2, 8)] if before is None else [(2, Q_DEV), (4,)]
    return pl.pallas_call(
        functools.partial(giants_kernel, first),
        grid=(POINTS_DEV // CHUNK,),
        in_specs=[lanes(9, 2) if first == 1 else lanes(24)] * 4
        + [whole(factors), lanes(7, 3, 2, 8)]
        + [lanes(2, 8) for _ in more],
        out_specs=[lanes(*shape) for shape in shapes],
        out_shape=[jax.ShapeDtypeStruct(shape + (POINTS_DEV,), F32) for shape in shapes],
        scratch_shapes=[pltpu.VMEM((96, CHUNK), F32)] * (2 if first == 1 else 1),
        compiler_params=pltpu.CompilerParams(vmem_limit_bytes=VMEM_BYTES),
        cost_estimate=pl.CostEstimate(flops=20000000, bytes_accessed=2000000, transcendentals=0),
    )(*parts, factors, keys, *more)


def lower_kernel(
    place_ref, total_ref, spare0_ref, spare1_ref, spare2_ref, spare3_ref, down_ref,
    zero_ref, rest0_ref, rest1_ref, rest2_ref, rest3_ref, out_ref,
):
    columns = down_columns(place_ref, down_ref)
    spares = (spare0_ref, spare1_ref, spare2_ref, spare3_ref)

    def piece(p, at):
        here = slice(at, at + LANES)
        rows = lambda m, i: spares[m][2 * p + i : 2 * p + i + 1, here]
        value = total_ref[p, :, here]
        if p == 0:
            for rest in (rest0_ref, rest1_ref, rest2_ref, rest3_ref):
                value = value + rest[:, here]
        else:
            value = value + zero_ref[:, here]
        return lowered(value, rows, columns)

    spread_rows(piece, out_ref)


def lower_call(place, total, spares, down, zero, rests):
    out = (SLOTS, Q_DEV, LANES)
    return pl.pallas_call(
        lower_kernel,
        in_specs=[PLACE] + [pl.BlockSpec(memory_space=pltpu.VMEM)] * 11,
        out_specs=pl.BlockSpec(memory_space=pltpu.VMEM),
        out_shape=jax.ShapeDtypeStruct(out, F32),
        compiler_params=pltpu.CompilerParams(vmem_limit_bytes=VMEM_BYTES),
        cost_estimate=pl.CostEstimate(flops=1000000, bytes_accessed=400000, transcendentals=0),
    )(place, total, *spares, down, zero, *rests)


def inverse_columns_kernel(in_ref, table_ref, out_ref, hold_ref):
    result = column_transform(in_ref, table_ref, hold_ref)
    for h in range(2):
        parts = [result[i][:, h * LANES : (h + 1) * LANES] for i in range(16)]
        for g, part in enumerate(exchange(parts, (6, 5, 4, 3))):
            out_ref[h * 16 + g] = part[:Q_DEV]


def inverse_rows_kernel(in_ref, table_ref, out_ref, hold_ref):
    hold_ref[...] = jnp.zeros_like(hold_ref)
    for h in range(2):
        parts = exchange([in_ref[h * 16 + c] for c in range(16)], (6, 2, 1, 0))
        for i, part in enumerate(parts):
            hold_ref[i, 0:Q_DEV, h * LANES : (h + 1) * LANES] = part
    result = transform(hold_ref[...].reshape(128, SIDE), table_ref).reshape(16, 8, SIDE)
    for p in range(2):
        for r in range(8):
            out_ref[0, :, p, r * SIDE : (r + 1) * SIDE] = result[p * 8 + r][:Q_DEV]


def swap(values, axis):
    return lax.all_to_all(values, axis, split_axis=0, concat_axis=0, tiled=True)


def shifted(block, distance):
    route = [(i, (i + distance) % SLOTS) for i in range(SLOTS)]
    return lax.ppermute(block, "slot", route)


def forward(ciphertexts):
    col_fwd, row_fwd, _, _ = dct_constants()
    hold = [pltpu.VMEM((16, 8, SIDE), F32)]
    parts = jnp.transpose(ciphertexts, (0, 2, 1, 3))
    sent = call(rows_kernel, [(SLOTS, Q_DEV, LANES)], parts)
    held = swap(sent, "slot")
    sent = call(
        columns_kernel, [(SLOTS, 2, Q_DEV, LANES)], held, col_fwd, scratch=hold, flops=50000000
    )
    held = swap(sent, "slot")
    shapes = [[(Q_DEV, HALO)], [(Q_DEV, HALO), (3, 2, HALO)]]
    e0, second = [
        call(
            functools.partial(evals_kernel, poly),
            shapes[poly],
            held,
            row_fwd,
            scratch=hold,
            flops=50000000,
        )
        for poly in range(2)
    ]
    return e0, *second


def inverse(sent):
    _, _, col_inv, row_inv = dct_constants()
    hold = [pltpu.VMEM((16, 8, SIDE), F32)]
    held = swap(sent, "slot")
    sent = call(
        inverse_columns_kernel,
        [(SLOTS, Q_DEV, LANES)],
        held,
        col_inv,
        scratch=hold,
        flops=50000000,
    )
    held = swap(sent, "slot")
    out = call(
        inverse_rows_kernel,
        [(1, Q_DEV, 2, POINTS_DEV)],
        held,
        row_inv,
        scratch=hold,
        flops=50000000,
    )
    return jnp.transpose(out, (0, 2, 1, 3))


def gathered(block):
    routes = [[(i, (i + m) % GROUPS) for i in range(GROUPS)] for m in range(GROUPS)]
    return [block] + [lax.ppermute(block, "limb", routes[m]) for m in range(1, GROUPS)]


def after(values, others):
    return lax.optimization_barrier((*values, *others))[: len(values)]


def together(*groups):
    flat = lax.optimization_barrier([value for group in groups for value in group])
    return [[flat.pop(0) for _ in group] for group in groups]


def per_device(ciphertexts, diagonals, baby_keys, giant_keys, up, down):
    place = lax.axis_index("limb").astype(jnp.int32).reshape(1)
    e0, e1, sent = forward(ciphertexts)
    evals = [e1] + gathered(sent)[1:]
    (late_up,), _ = together([up], [e1])
    factors, giant_factors = factors_call(place, late_up)
    kept, spare0, spare1 = products_call(evals, factors, baby_keys)
    *sends, zero, four = babies_call(1, place, kept, gathered(spare1), e1, down, diagonals)
    spares0 = gathered(spare0)
    gots = [shifted(send, r + 1) for r, send in enumerate(sends)]
    sums = babies_call(0, place, kept, spares0, e0, down, diagonals)
    low, high = sums
    gots, (low,) = together(gots, [low])
    shapes = [(9, 2, POINTS_DEV), (24, POINTS_DEV)]
    near, far = call(sort_kernel, shapes, *gots, four, flops=10000)
    far = shifted(far, 4)
    high = shifted(high, 4)
    nears = gathered(near)
    nears[1:], (far,) = together(nears[1:], [far])
    (before,) = giants_call(1, nears, giant_factors, giant_keys)
    (high,), (before,) = together([high], [before])
    rests = call(pair_sum_kernel, [(Q_DEV, POINTS_DEV)] * 4, low, high, flops=10000)
    rests = [rests[0]] + [shifted(rests[r], r) for r in range(1, 4)]
    total, spare = giants_call(4, gathered(far), giant_factors, giant_keys, before)
    return inverse(lower_call(place, total, gathered(spare), down, zero, rests))


def solution(mesh):
    placed = (
        P("ct", None, "limb", "slot"),
        P(None, None, "limb", "slot"),
        P(None, None, None, "limb", "slot"),
        P(None, None, None, "limb", "slot"),
        P("limb", None),
        P("limb", None),
    )
    return jax.shard_map(
        per_device,
        mesh=mesh,
        in_specs=placed,
        out_specs=P("ct", None, "limb", "slot"),
        check_vma=False,
    )
```

```python
import functools

import numpy as np
import jax
import jax.numpy as jnp
import ml_dtypes
from jax import lax
from jax.experimental import pallas as pl
from jax.experimental.pallas import tpu as pltpu
from jax.sharding import PartitionSpec as P

SIDE = 256
DNUM = 3
BABY = 8
GIANT = 8
Q_DEV = 6
LANES = 128
POINTS_DEV = 2048
HALO = 2 * POINTS_DEV
SLOTS = 32
GROUPS = 4
CHUNK = 2048
VMEM_BYTES = 28 * 1024 * 1024
F32 = jnp.float32
BF16 = jnp.bfloat16


def split_constant(values):
    high = values.astype(ml_dtypes.bfloat16)
    low = (values - high.astype(np.float64)).astype(ml_dtypes.bfloat16)
    return np.stack([high, low])


def cosine_matrix():
    k = np.arange(SIDE, dtype=np.float64)[:, None]
    n = np.arange(SIDE, dtype=np.float64)[None, :]
    scale = np.where(k == 0, np.sqrt(1.0 / SIDE), np.sqrt(2.0 / SIDE))
    return scale * np.cos(np.pi * (n + 0.5) * k / SIDE)


def lane_orders():
    lane = np.arange(SIDE)
    half, low = lane // LANES, lane % LANES
    block, rest = low // 64, low % 64
    rows = half * 128 + block * 64 + (rest % 8) * 8 + rest // 8
    cols_fwd = half * 128 + (low % 16) * 8 + low // 16
    c = (low // 64) * 8 + low % 8
    k = (low // 8) % 8
    cols_inv = half * 128 + c * 8 + k
    return rows, cols_fwd, cols_inv


def dct_constants():
    c = cosine_matrix()
    rows, cols_fwd, cols_inv = lane_orders()
    return (
        split_constant(c.T[rows]),
        split_constant(c.T[cols_fwd]),
        split_constant(c[rows]),
        split_constant(c[cols_inv]),
    )


def exchange(values, bits, axis=1):
    values = list(values)
    size = values[0].shape[axis]
    index = lax.broadcasted_iota(jnp.int32, values[0].shape, axis)
    for place, bit in enumerate(reversed(bits)):
        step, span = 1 << place, 1 << bit
        keep = (index & span) == 0
        for i in range(len(values)):
            if i & step:
                continue
            a, b = values[i], values[i + step]
            values[i] = jnp.where(keep, a, pltpu.roll(b, span, axis))
            values[i + step] = jnp.where(keep, pltpu.roll(a, size - span, axis), b)
    return values


def halves(values):
    high = values.astype(BF16)
    return high, (values - high.astype(F32)).astype(BF16)


def matmul(a, b):
    return lax.dot_general(a, b, (((1,), (0,)), ((), ())), preferred_element_type=F32)


def exact_matmul(a, b):
    return lax.dot_general(
        a,
        b,
        (((1,), (0,)), ((), ())),
        precision=lax.Precision.HIGHEST,
        preferred_element_type=F32,
    )


def transform(values, table):
    high, low = halves(values)
    return matmul(high, table[0]) + matmul(low, table[0]) + matmul(high, table[1])


def call(kernel, out_shapes, *args, scratch=(), flops=1000000):
    shapes = [jax.ShapeDtypeStruct(s, F32) for s in out_shapes]
    return pl.pallas_call(
        kernel,
        out_shape=shapes if len(shapes) > 1 else shapes[0],
        scratch_shapes=list(scratch),
        compiler_params=pltpu.CompilerParams(vmem_limit_bytes=VMEM_BYTES),
        cost_estimate=pl.CostEstimate(flops=flops, bytes_accessed=400000, transcendentals=0),
    )(*args)


def group_of(place_ref, m):
    return (place_ref[0] - m) & 3


def down_columns(place_ref, down_ref):
    down = down_ref[...]
    lane = lax.broadcasted_iota(jnp.int32, down.shape, 1)
    columns = []
    for m in range(GROUPS):
        for i in range(2):
            pick = jnp.where(lane == 2 * group_of(place_ref, m) + i, down, 0.0)
            column = jnp.sum(pick, axis=1, keepdims=True)
            columns.append(jnp.broadcast_to(column, (Q_DEV, LANES)))
    return columns


def lowered(kept, rows, columns):
    total = kept
    for g in range(GROUPS):
        for i in range(2):
            total = total - columns[2 * g + i] * rows(g, i)
    return total


def spread_rows(piece, out_ref):
    for h in range(2):
        parts = [piece(p, r * SIDE + h * LANES) for p in range(2) for r in range(8)]
        for c, part in enumerate(exchange(parts, (6, 5, 4, 3))):
            out_ref[h * 16 + c] = part


def rows_kernel(x_ref, out_ref):
    spread_rows(lambda p, at: x_ref[0, :, p, at : at + LANES], out_ref)


def column_transform(in_ref, table_ref, hold_ref):
    hold_ref[...] = jnp.zeros_like(hold_ref)
    for h in range(2):
        parts = exchange([in_ref[h * 16 + s] for s in range(16)], (6, 2, 1, 0))
        for i, part in enumerate(parts):
            hold_ref[i, 0:Q_DEV, h * LANES : (h + 1) * LANES] = part
    result = transform(hold_ref[...].reshape(128, SIDE), table_ref)
    return result.reshape(16, 8, SIDE)


def columns_kernel(in_ref, table_ref, out_ref, hold_ref):
    result = column_transform(in_ref, table_ref, hold_ref)
    lane = lax.broadcasted_iota(jnp.int32, (8, LANES), 1)
    first = (lane & 8) == 0
    for p in range(2):
        pairs = []
        for h in range(2):
            parts = [result[p * 8 + k][:, h * LANES : (h + 1) * LANES] for k in range(8)]
            pairs += exchange(parts, (6, 5, 4))
        for i in range(16):
            out_ref[2 * i + 1, p] = pairs[i][:Q_DEV]
            both = jnp.where(
                first, pltpu.roll(pairs[i - 1], LANES - 8, 1), pltpu.roll(pairs[i], 8, 1)
            )
            out_ref[2 * i, p] = both[:Q_DEV]


def evals_kernel(poly, in_ref, table_ref, *refs):
    *out_refs, hold_ref = refs
    hold_ref[...] = jnp.zeros_like(hold_ref)
    for h in range(2):
        parts = exchange([in_ref[h * 16 + c, poly] for c in range(16)], (3, 2, 1, 0))
        for row, part in enumerate(parts):
            hold_ref[row, 0:Q_DEV, h * LANES : (h + 1) * LANES] = part
    result = transform(hold_ref[...].reshape(128, SIDE), table_ref).reshape(16, 8, SIDE)
    for row in range(16):
        at = slice(row * SIDE, (row + 1) * SIDE)
        out_refs[0][:, at] = result[row][:Q_DEV]
        if poly == 1:
            for i in range(3):
                out_refs[1][i, :, at] = result[row][2 * i : 2 * i + 2]


def factors_kernel(place_ref, up_ref, baby_ref, giant_ref):
    iota = lambda shape, axis: lax.broadcasted_iota(jnp.int32, shape, axis)
    up = up_ref[...]

    def spread(held, limb, columns):
        pick = (iota((24, columns), 0) == limb).astype(F32)
        wide = exact_matmul(up, pick)
        digit = limb[0:8] >> 3
        return [jnp.where(held[0:8] & (digit == d), wide, 0.0) for d in range(DNUM)]

    q = iota((24, 32), 1)
    used = (q & 7) < Q_DEV
    limb = jnp.where(used, 6 * group_of(place_ref, q >> 3) + (q & 7), -8)
    fh, fl = halves(jnp.concatenate(spread(used, limb, 32), axis=0))
    baby_ref[...] = jnp.concatenate([fh, fh, fl], axis=1).astype(F32)
    q = iota((24, 96), 1)
    block = (q >= 24).astype(jnp.int32) + (q >= 48) + (q >= 72)
    rest = q - 24 * block
    giant = (rest * 43) >> 8
    limb = 6 * group_of(place_ref, block) + rest - 6 * giant
    for j in range(4):
        at = slice(j * 24, j * 24 + 24)
        fh, fl = halves(jnp.concatenate(spread(giant == j, limb, 96), axis=0))
        giant_ref[0, at], giant_ref[1, at] = fh.astype(F32), fl.astype(F32)


def factors_call(place, up):
    return pl.pallas_call(
        factors_kernel,
        in_specs=[pl.BlockSpec(memory_space=pltpu.SMEM), pl.BlockSpec(memory_space=pltpu.VMEM)],
        out_specs=[pl.BlockSpec(memory_space=pltpu.VMEM)] * 2,
        out_shape=[
            jax.ShapeDtypeStruct((24, 96), F32),
            jax.ShapeDtypeStruct((2, 96, 96), F32),
        ],
        compiler_params=pltpu.CompilerParams(vmem_limit_bytes=VMEM_BYTES),
        cost_estimate=pl.CostEstimate(flops=1000000, bytes_accessed=100000, transcendentals=0),
    )(place, up)


def products_kernel(
    e1a_ref, e1b_ref, e1c_ref, e1d_ref, factors_ref, keys_ref,
    kept_ref, spare0_ref, spare1_ref, raised_ref, stage_ref,
):
    step = pl.program_id(0)

    @pl.when(step == 0)
    def _():
        lhs = factors_ref[...].astype(BF16)
        stage_ref[...] = jnp.zeros_like(stage_ref)
        stage_ref[0:Q_DEV, :] = e1a_ref[...]
        for m, ref in enumerate((e1b_ref, e1c_ref, e1d_ref), 1):
            for i in range(3):
                stage_ref[8 * m + 2 * i : 8 * m + 2 * i + 2, :] = ref[i]
        for part in range(8):
            at = slice(part * 512, (part + 1) * 512)
            eh, el = halves(stage_ref[:, at])
            raised_ref[:, at] = matmul(lhs, jnp.concatenate([eh, el, eh], axis=0))

    spares = (spare0_ref, spare1_ref)

    def body(t, carry):
        base = pl.multiple_of(step * CHUNK + t * LANES, LANES)
        here = pl.ds(pl.multiple_of(t * LANES, LANES), LANES)
        for k in range(1, BABY):
            at = pl.ds(base + (8 - k) * SIDE, LANES)
            views = [raised_ref[d * 8 : d * 8 + 8, at] for d in range(DNUM)]
            for s in range(2):
                total = None
                for d in range(DNUM):
                    term = views[d] * keys_ref[k - 1, d, s, :, here].astype(F32)
                    total = term if total is None else total + term
                kept_ref[s, k - 1, :, here] = total
                spares[s][k - 1, :, here] = total[Q_DEV:]
        return carry

    lax.fori_loop(0, CHUNK // LANES, body, 0)


def babies_kernel(
    poly, place_ref, kept_ref, spare0_ref, spare1_ref, spare2_ref, spare3_ref,
    evals_ref, down_ref, diag_ref, *out_refs,
):
    step = pl.program_id(0)
    columns = down_columns(place_ref, down_ref)
    spares = (spare0_ref, spare1_ref, spare2_ref, spare3_ref)

    def body(t, carry):
        base = pl.multiple_of(step * CHUNK + t * LANES, LANES)
        here = pl.ds(pl.multiple_of(t * LANES, LANES), LANES)
        babies = [evals_ref[:, pl.ds(base + POINTS_DEV, LANES)]]
        for k in range(1, BABY):
            rows = lambda m, i: spares[m][k - 1, i : i + 1, here]
            baby = lowered(kept_ref[0, k - 1, 0:Q_DEV, here], rows, columns)
            if poly == 0:
                baby = baby + evals_ref[:, pl.ds(base + (8 - k) * SIDE, LANES)]
            babies.append(baby)
        for j in range(GIANT):
            inner = None
            for k in range(BABY):
                term = diag_ref[j, k, :, here].astype(F32) * babies[k]
                inner = term if inner is None else inner + term
            if poly == 0:
                at = 6 * (j % 4)
                out_refs[j // 4][at : at + 6, here] = inner
            elif j % 4 == 0:
                out_refs[3 + j // 4][:, here] = inner
            else:
                for i in range(3):
                    out_refs[j % 4 - 1][3 * (j // 4) + i, :, here] = inner[2 * i : 2 * i + 2]
        return carry

    lax.fori_loop(0, CHUNK // LANES, body, 0)


def whole(a):
    return pl.BlockSpec(a.shape, lambda i, n=a.ndim: (0,) * n)


def lanes(*lead):
    return pl.BlockSpec(lead + (CHUNK,), lambda i, n=len(lead): (0,) * n + (i,))


PLACE = pl.BlockSpec(memory_space=pltpu.SMEM)


def products_call(evals, factors, keys):
    return pl.pallas_call(
        products_kernel,
        grid=(POINTS_DEV // CHUNK,),
        in_specs=[whole(e) for e in evals] + [whole(factors), lanes(7, 3, 2, 8)],
        out_specs=[lanes(2, 7, 8), lanes(7, 2), lanes(7, 2)],
        out_shape=[
            jax.ShapeDtypeStruct((2, 7, 8, POINTS_DEV), F32),
            jax.ShapeDtypeStruct((7, 2, POINTS_DEV), F32),
            jax.ShapeDtypeStruct((7, 2, POINTS_DEV), F32),
        ],
        scratch_shapes=[pltpu.VMEM((24, HALO), F32), pltpu.VMEM((32, HALO), F32)],
        compiler_params=pltpu.CompilerParams(vmem_limit_bytes=VMEM_BYTES),
        cost_estimate=pl.CostEstimate(flops=40000000, bytes_accessed=4000000, transcendentals=0),
    )(*evals, factors, keys)


def babies_call(poly, place, kept, spares, evals, down, diagonals):
    rows = [(24,), (24,)] if poly == 0 else [(6, 2)] * 3 + [(6,)] * 2
    part = pl.BlockSpec((1, 7, 8, CHUNK), lambda i: (poly, 0, 0, i))
    return pl.pallas_call(
        functools.partial(babies_kernel, poly),
        grid=(POINTS_DEV // CHUNK,),
        in_specs=[PLACE, part]
        + [lanes(7, 2)] * 4
        + [whole(evals), whole(down), lanes(8, 8, Q_DEV)],
        out_specs=[lanes(*r) for r in rows],
        out_shape=[jax.ShapeDtypeStruct((*r, POINTS_DEV), F32) for r in rows],
        compiler_params=pltpu.CompilerParams(vmem_limit_bytes=VMEM_BYTES),
        cost_estimate=pl.CostEstimate(flops=40000000, bytes_accessed=6000000, transcendentals=0),
    )(place, kept, *spares, evals, down, diagonals)


def sort_kernel(got1_ref, got2_ref, got3_ref, four_ref, near_ref, far_ref):
    far_ref[0:6, :] = four_ref[...]
    for r, got in enumerate((got1_ref, got2_ref, got3_ref)):
        for i in range(3):
            near_ref[3 * r + i] = got[i]
            far_ref[6 + 6 * r + 2 * i : 8 + 6 * r + 2 * i, :] = got[3 + i]


def pair_sum_kernel(low_ref, high_ref, *out_refs):
    for r, out_ref in enumerate(out_refs):
        for i in range(3):
            at = slice(6 * r + 2 * i, 6 * r + 2 * i + 2)
            out_ref[i] = low_ref[at, :] + high_ref[at, :]


def giants_kernel(
    first, part0_ref, part1_ref, part2_ref, part3_ref, factor_ref, keys_ref, *refs
):
    before_ref = spare_ref = None
    if first == 1:
        total_ref, raised_ref, stage_ref = refs
    else:
        before_ref, total_ref, spare_ref, raised_ref = refs
    fh, fl = factor_ref[0].astype(BF16), factor_ref[1].astype(BF16)
    parts = (part0_ref, part1_ref, part2_ref, part3_ref)
    if first == 1:
        for m, ref in enumerate(parts):
            for i in range(9):
                stage_ref[24 * m + 2 * i : 24 * m + 2 * i + 2, :] = ref[i]
            stage_ref[24 * m + 18 : 24 * m + 24, :] = jnp.zeros((6, CHUNK), F32)
        held = stage_ref[...]
    else:
        held = jnp.concatenate([ref[...] for ref in parts], axis=0)
    eh, el = halves(held)
    raised_ref[...] = matmul(fh, eh) + matmul(fh, el) + matmul(fl, eh)

    def body(t, carry):
        here = pl.ds(pl.multiple_of(t * LANES, LANES), LANES)
        sums = [None, None]
        if before_ref is not None:
            sums = [before_ref[s, :, here] for s in range(2)]
        for j in range(3 if first == 1 else 4):
            for d in range(DNUM):
                at = j * 24 + d * 8
                value = raised_ref[at : at + 8, here]
                for s in range(2):
                    key = keys_ref[first - 1 + j, d, s, :, here].astype(F32)
                    sums[s] = value * key if sums[s] is None else sums[s] + value * key
        if before_ref is None:
            total_ref[0, :, here], total_ref[1, :, here] = sums
        else:
            for s in range(2):
                total_ref[s, :, here] = sums[s][:Q_DEV]
                spare_ref[2 * s : 2 * s + 2, here] = sums[s][Q_DEV:]
        return carry

    lax.fori_loop(0, CHUNK // LANES, body, 0)


def giants_call(first, parts, factors, keys, before=None):
    more = [] if before is None else [before]
    shapes = [(2, 8)] if before is None else [(2, Q_DEV), (4,)]
    return pl.pallas_call(
        functools.partial(giants_kernel, first),
        grid=(POINTS_DEV // CHUNK,),
        in_specs=[lanes(9, 2) if first == 1 else lanes(24)] * 4
        + [whole(factors), lanes(7, 3, 2, 8)]
        + [lanes(2, 8) for _ in more],
        out_specs=[lanes(*shape) for shape in shapes],
        out_shape=[jax.ShapeDtypeStruct(shape + (POINTS_DEV,), F32) for shape in shapes],
        scratch_shapes=[pltpu.VMEM((96, CHUNK), F32)] * (2 if first == 1 else 1),
        compiler_params=pltpu.CompilerParams(vmem_limit_bytes=VMEM_BYTES),
        cost_estimate=pl.CostEstimate(flops=20000000, bytes_accessed=2000000, transcendentals=0),
    )(*parts, factors, keys, *more)


def lower_kernel(
    place_ref, total_ref, spare0_ref, spare1_ref, spare2_ref, spare3_ref, down_ref,
    zero_ref, rest0_ref, rest1_ref, rest2_ref, rest3_ref, out_ref,
):
    columns = down_columns(place_ref, down_ref)
    spares = (spare0_ref, spare1_ref, spare2_ref, spare3_ref)

    def piece(p, at):
        here = slice(at, at + LANES)
        rows = lambda m, i: spares[m][2 * p + i : 2 * p + i + 1, here]
        value = total_ref[p, :, here]
        if p == 0:
            for rest in (rest0_ref, rest1_ref, rest2_ref, rest3_ref):
                value = value + jnp.concatenate([rest[i, :, here] for i in range(3)], axis=0)
        else:
            value = value + zero_ref[:, here]
        return lowered(value, rows, columns)

    spread_rows(piece, out_ref)


def lower_call(place, total, spares, down, zero, rests):
    out = (SLOTS, Q_DEV, LANES)
    return pl.pallas_call(
        lower_kernel,
        in_specs=[PLACE] + [pl.BlockSpec(memory_space=pltpu.VMEM)] * 11,
        out_specs=pl.BlockSpec(memory_space=pltpu.VMEM),
        out_shape=jax.ShapeDtypeStruct(out, F32),
        compiler_params=pltpu.CompilerParams(vmem_limit_bytes=VMEM_BYTES),
        cost_estimate=pl.CostEstimate(flops=1000000, bytes_accessed=400000, transcendentals=0),
    )(place, total, *spares, down, zero, *rests)


def inverse_columns_kernel(in_ref, table_ref, out_ref, hold_ref):
    result = column_transform(in_ref, table_ref, hold_ref)
    for h in range(2):
        parts = [result[i][:, h * LANES : (h + 1) * LANES] for i in range(16)]
        for g, part in enumerate(exchange(parts, (6, 5, 4, 3))):
            out_ref[h * 16 + g] = part[:Q_DEV]


def inverse_rows_kernel(in_ref, table_ref, out_ref, hold_ref):
    hold_ref[...] = jnp.zeros_like(hold_ref)
    for h in range(2):
        parts = exchange([in_ref[h * 16 + c] for c in range(16)], (6, 2, 1, 0))
        for i, part in enumerate(parts):
            hold_ref[i, 0:Q_DEV, h * LANES : (h + 1) * LANES] = part
    result = transform(hold_ref[...].reshape(128, SIDE), table_ref).reshape(16, 8, SIDE)
    for p in range(2):
        for r in range(8):
            out_ref[0, :, p, r * SIDE : (r + 1) * SIDE] = result[p * 8 + r][:Q_DEV]


def swap(values, axis):
    return lax.all_to_all(values, axis, split_axis=0, concat_axis=0, tiled=True)


def shifted(block, distance):
    route = [(i, (i + distance) % SLOTS) for i in range(SLOTS)]
    return lax.ppermute(block, "slot", route)


def forward(ciphertexts):
    col_fwd, row_fwd, _, _ = dct_constants()
    hold = [pltpu.VMEM((16, 8, SIDE), F32)]
    parts = jnp.transpose(ciphertexts, (0, 2, 1, 3))
    sent = call(rows_kernel, [(SLOTS, Q_DEV, LANES)], parts)
    held = swap(sent, "slot")
    sent = call(
        columns_kernel, [(SLOTS, 2, Q_DEV, LANES)], held, col_fwd, scratch=hold, flops=50000000
    )
    held = swap(sent, "slot")
    shapes = [[(Q_DEV, HALO)], [(Q_DEV, HALO), (3, 2, HALO)]]
    e0, second = [
        call(
            functools.partial(evals_kernel, poly),
            shapes[poly],
            held,
            row_fwd,
            scratch=hold,
            flops=50000000,
        )
        for poly in range(2)
    ]
    return e0, *second


def inverse(sent):
    _, _, col_inv, row_inv = dct_constants()
    hold = [pltpu.VMEM((16, 8, SIDE), F32)]
    held = swap(sent, "slot")
    sent = call(
        inverse_columns_kernel,
        [(SLOTS, Q_DEV, LANES)],
        held,
        col_inv,
        scratch=hold,
        flops=50000000,
    )
    held = swap(sent, "slot")
    out = call(
        inverse_rows_kernel,
        [(1, Q_DEV, 2, POINTS_DEV)],
        held,
        row_inv,
        scratch=hold,
        flops=50000000,
    )
    return jnp.transpose(out, (0, 2, 1, 3))


def gathered(block):
    routes = [[(i, (i + m) % GROUPS) for i in range(GROUPS)] for m in range(GROUPS)]
    return [block] + [lax.ppermute(block, "limb", routes[m]) for m in range(1, GROUPS)]


def after(values, others):
    return lax.optimization_barrier((*values, *others))[: len(values)]


def together(*groups):
    flat = lax.optimization_barrier([value for group in groups for value in group])
    return [[flat.pop(0) for _ in group] for group in groups]


def per_device(ciphertexts, diagonals, baby_keys, giant_keys, up, down):
    place = lax.axis_index("limb").astype(jnp.int32).reshape(1)
    e0, e1, sent = forward(ciphertexts)
    evals = [e1] + gathered(sent)[1:]
    (late_up,), _ = together([up], [e1])
    factors, giant_factors = factors_call(place, late_up)
    kept, spare0, spare1 = products_call(evals, factors, baby_keys)
    *sends, zero, four = babies_call(1, place, kept, gathered(spare1), e1, down, diagonals)
    spares0 = gathered(spare0)
    gots = [shifted(send, r + 1) for r, send in enumerate(sends)]
    sums = babies_call(0, place, kept, spares0, e0, down, diagonals)
    low, high = sums
    gots, (low,) = together(gots, [low])
    shapes = [(9, 2, POINTS_DEV), (24, POINTS_DEV)]
    near, far = call(sort_kernel, shapes, *gots, four, flops=10000)
    far = shifted(far, 4)
    high = shifted(high, 4)
    nears = gathered(near)
    nears[1:], (far,) = together(nears[1:], [far])
    (before,) = giants_call(1, nears, giant_factors, giant_keys)
    (high,), (before,) = together([high], [before])
    rests = call(pair_sum_kernel, [(3, 2, POINTS_DEV)] * 4, low, high, flops=10000)
    rests = [rests[0]] + [shifted(rests[r], r) for r in range(1, 4)]
    total, spare = giants_call(4, gathered(far), giant_factors, giant_keys, before)
    return inverse(lower_call(place, total, gathered(spare), down, zero, rests))


def solution(mesh):
    placed = (
        P("ct", None, "limb", "slot"),
        P(None, None, "limb", "slot"),
        P(None, None, None, "limb", "slot"),
        P(None, None, None, "limb", "slot"),
        P("limb", None),
        P("limb", None),
    )
    return jax.shard_map(
        per_device,
        mesh=mesh,
        in_specs=placed,
        out_specs=P("ct", None, "limb", "slot"),
        check_vma=False,
    )
```
